32 devices in a mesh: grp: 2 (over x), head: 8 (over z, y), item: 2 (over core).
Axes of the slice: x: 2, y: 2, z: 4, core: 2. Of those that a mesh axis runs over, the one named last changes fastest.
Arguments:
- passage_states: bfloat16 [4096, 8192], P(('grp', 'item'), 'head'), parts along dimension 0
- question_states: bfloat16 [2048, 8192], P(('grp', 'item'), 'head'), parts along dimension 0
- norm_gain: float32 [8192], P('head'), may hold values from 0.1 to 1.9
- query_weight: bfloat16 [8192, 8192], P(None, 'head')
- kv_weight: bfloat16 [8192, 2048], P('head')
- out_weight: bfloat16 [8192, 8192], P('head'), may hold values from -0.09375 to 0.09375
- passage_ids: int32 [16, 4], P(('grp', 'item')), parts along dimension 0, may hold values from 0 to 7, all different within a row
- slot_offsets: int32 [16, 4], P(('grp', 'item')), parts along dimension 0, may hold values from 0 to 768
Outputs:
- passage_kv: bfloat16 [4096, 2048], P(('grp', 'item'), 'head'), parts along dimension 0
- question_out: bfloat16 [2048, 8192], P(('grp', 'item'), 'head'), parts along dimension 0
The draws below stay inside these ranges and needn't reach their ends.
There are 2 independent parts, one for each index of `grp`. The reference program is written for one: setup_inputs(seed, part) draws one part's arguments, and reference() takes and returns one part's arrays. A program takes and returns all parts, laid end to end along the dimension named above; an argument that names none is the same for every part. Nothing has to cross between parts.
Inputs may be any that keep to these rules, and one draw needn't show every extreme that they name: `passage_ids`: each request names 4 different passages and every passage is named by some request.
All inputs are finite; a program needn't handle non-finite values.
Results may differ from the reference program's by a relative error of at most 0.0055.
Values may be sent and summed in bfloat16 or wider, within the bound.
No kernel may reach another device: no remote copies, remote signals or barrier semaphores. Data moves between devices by JAX's collectives and lax.ppermute only.
A program may use at most 192 MiB of HBM per device.

```python
import math
import jax
import jax.numpy as jnp
from jax import lax

D = 8192
HEADS = 64
KV_HEADS = 8
HD = 128
PLEN = 256
QLEN = 128
SLOTS = 4
PASSAGES = 8
REQUESTS = 8


def key_columns(key):
    return jax.random.normal(key, (D, 2 * KV_HEADS * HD), jnp.float32) * D ** (-0.5)


def draw_passage_states(key, part):
    key = jax.random.fold_in(key, 5)
    key_base, key_cols = jax.random.split(key, 2)
    row_total = PASSAGES * PLEN
    col_scale = jnp.exp(jax.random.uniform(key_cols, (D,), jnp.float32, -1.2, 1.2))
    result = jax.random.normal(key_base, (row_total, D), jnp.float32) * col_scale[None, :]
    return result.astype(jnp.bfloat16)


def draw_question_states(key, part):
    key = jax.random.fold_in(key, 9)
    key_base, key_cols = jax.random.split(key, 2)
    row_total = REQUESTS * QLEN
    col_scale = jnp.exp(jax.random.uniform(key_cols, (D,), jnp.float32, -1.2, 1.2))
    result = jax.random.normal(key_base, (row_total, D), jnp.float32) * col_scale[None, :]
    return result.astype(jnp.bfloat16)


def draw_kv_weight(key, part):
    common = key_columns(key)
    return common.astype(jnp.bfloat16)


def draw_query_weight(key, part):
    key = jax.random.fold_in(key, 7)
    key_noise = jax.random.fold_in(key, 0)
    noise = jax.random.normal(key_noise, (D, HEADS * HD), jnp.float32) * D ** (-0.5)
    result = noise
    return result.astype(jnp.bfloat16)


def plant(values, stream_key, smallest, top_value):
    extent = values.shape
    index_at = [jax.random.randint(jax.random.fold_in(stream_key, axis), (), 0, extent[axis]) for axis in range(len(extent))]
    values = values.at[tuple(index_at)].set(smallest)
    longest = extent.index(max(extent))
    index_at[longest] = (index_at[longest] + 1) % extent[longest]
    return values.at[tuple(index_at)].set(top_value)


def raised(values, key, source, target, blocks, factor):
    def block_of(position):
        return (jnp.arange(values.shape[position]) // (values.shape[position] // blocks)).reshape((-1,) + (1,) * (values.ndim - 1 - position))

    first = jax.random.permutation(key, blocks)[block_of(target)]
    second = (block_of(target) + blocks // 2) % blocks
    return jnp.where((block_of(source) == first) | (block_of(source) == second), factor * values, values)


def shard_levels(key, extent, pieces, smallest, top_value):
    level = 1.0
    for position, shards_of in pieces:
        draws = jax.random.uniform(jax.random.fold_in(jax.random.fold_in(key, 6), position), (shards_of,), jnp.float32, smallest / len(pieces), top_value / len(pieces))
        level = level * jnp.repeat(jnp.exp(draws), extent[position] // shards_of).reshape((-1,) + (1,) * (len(extent) - 1 - position))
    return level


def distinct(stream_key, rows, count, top, lift):
    order = jax.random.permutation(jax.random.fold_in(stream_key, 1), count)
    favour = order
    for power in range(3):
        favour = favour * favour // count
    favour = favour * lift // count
    lots = jax.random.randint(jax.random.fold_in(stream_key, 2), (rows, count), 0, 4096) + favour
    holders = jax.random.permutation(jax.random.fold_in(stream_key, 3), rows)[jnp.arange(count) % rows]
    lots = jnp.where(jnp.arange(rows)[:, None] == holders[None, :], 1 << 14, lots)
    priority = lots * count + jnp.arange(count)
    return lax.top_k(priority.astype(jnp.int32), top)[1].astype(jnp.int32)


def bell_draw_with(own_key, extent, deviation, bound, cuts, heavy, held_as=jnp.bfloat16):
    drawn = deviation * jax.random.normal(own_key, extent, jnp.float32)
    if cuts:
        drawn = drawn * shard_levels(own_key, extent, cuts, -0.22, 0.18)
    return jnp.clip(raised(drawn, jax.random.fold_in(own_key, 3), *heavy), -bound, bound).astype(held_as)


def setup_inputs(seed: int = 0, part: int = 0) -> dict:
    keys = jax.random.split(jax.random.key(seed), 9)
    own_keys = jax.random.split(jax.random.fold_in(keys[8], part), 9)
    return {
        "passage_states": draw_passage_states(jax.random.fold_in(jax.random.fold_in(keys[8], part), 71), part),
        "question_states": draw_question_states(jax.random.fold_in(jax.random.fold_in(keys[8], part), 71), part),
        "norm_gain": jnp.clip(1.0 + 0.18 * jax.random.normal(keys[2], (D,), jnp.float32), 0.1, 1.9),
        "query_weight": draw_query_weight(jax.random.fold_in(keys[8], 71), part),
        "kv_weight": draw_kv_weight(jax.random.fold_in(keys[8], 71), part),
        "out_weight": bell_draw_with(keys[5], (HEADS * HD, D), (HEADS * HD) ** -0.5, 0.09375, ((0, 8),), (0, 1, 8, 2.0)),
        "passage_ids": distinct(own_keys[6], REQUESTS, PASSAGES, SLOTS, 8192),
        "slot_offsets": plant(jax.random.randint(own_keys[7], (REQUESTS, SLOTS), 0, (SLOTS - 1) * PLEN + 1), jax.random.fold_in(own_keys[7], 1), 0, (SLOTS - 1) * PLEN).astype(jnp.int32),
    }


def rotate(matrix, positions):
    half_dim = matrix.shape[-1] // 2
    inverse = jnp.exp(jnp.arange(half_dim, dtype=jnp.float32) * (-2.0 * math.log(500000.0) / matrix.shape[-1]))
    angles = positions.astype(jnp.float32)[:, None] * inverse[None, :]
    cosine = jnp.cos(angles)
    sine_part = jnp.sin(angles)
    first_half = matrix[..., :half_dim]
    second = matrix[..., half_dim:]
    return jnp.concatenate([first_half * cosine - second * sine_part, second * cosine + first_half * sine_part], axis=-1)

def normed(states, norm_gain):
    values = states.astype(jnp.float32)
    row_scale = lax.rsqrt(lax.optimization_barrier(jnp.mean(values * values, axis=1, keepdims=True)) + 1e-05)
    return ((values * norm_gain[None, :]).astype(jnp.bfloat16), row_scale)

def attend(turned, key_rows, value_rows, question_len):
    scores = lax.dot_general(turned, key_rows, (((1,), (1,)), ((), ())), preferred_element_type=jnp.float32)
    key_count = key_rows.shape[0]
    cached = key_count - question_len
    row_pos = jnp.arange(turned.shape[0], dtype=jnp.int32) % question_len
    col_pos = jnp.arange(key_count, dtype=jnp.int32)
    allowed = (col_pos[None, :] < cached) | (col_pos[None, :] - cached <= row_pos[:, None])
    scores = jnp.where(allowed, scores, -1e+30)
    row_max = lax.optimization_barrier(jnp.max(scores, axis=1, keepdims=True))
    weights = jnp.where(allowed, jnp.exp(scores - row_max), 0.0)
    total_weight = lax.optimization_barrier(jnp.sum(weights, axis=1, keepdims=True))
    blended = jnp.dot(weights.astype(jnp.bfloat16), value_rows, preferred_element_type=jnp.float32)
    return blended / total_weight

def reference(passage_states, question_states, norm_gain, query_weight, kv_weight, out_weight, passage_ids, slot_offsets):
    gained_p, scale_p = normed(passage_states, norm_gain)
    passage_kv = (scale_p * jnp.dot(gained_p, kv_weight, preferred_element_type=jnp.float32)).astype(jnp.bfloat16)
    gained_q, scale_q = normed(question_states, norm_gain)
    question_kv = (scale_q * jnp.dot(gained_q, kv_weight, preferred_element_type=jnp.float32)).astype(jnp.bfloat16)
    queries = scale_q * jnp.dot(gained_q, query_weight, preferred_element_type=jnp.float32)
    stored_kv = passage_kv.reshape(PASSAGES, PLEN, KV_HEADS, 2, HD)
    group_heads = HEADS // KV_HEADS

    def one_request(inputs_one):
        request_q, request_kv, chosen, offsets = inputs_one
        q_pos = SLOTS * PLEN + jnp.arange(QLEN, dtype=jnp.int32)
        turned = rotate(jnp.transpose(request_q, (1, 0, 2)), q_pos) * HD ** (-0.5)
        turned = turned.astype(jnp.bfloat16).reshape(KV_HEADS, group_heads * QLEN, HD)
        picked = stored_kv[chosen].reshape(SLOTS * PLEN, KV_HEADS, 2, HD)
        p_pos = (offsets[:, None] + jnp.arange(PLEN, dtype=jnp.int32)[None, :]).reshape(SLOTS * PLEN)
        p_keys = rotate(jnp.transpose(picked[:, :, 0, :], (1, 0, 2)).astype(jnp.float32), p_pos)
        q_keys = rotate(jnp.transpose(request_kv[:, :, 0, :], (1, 0, 2)).astype(jnp.float32), q_pos)
        key_rows = jnp.concatenate([p_keys, q_keys], axis=1).astype(jnp.bfloat16)
        value_rows = jnp.concatenate([jnp.transpose(picked[:, :, 1, :], (1, 0, 2)), jnp.transpose(request_kv[:, :, 1, :], (1, 0, 2))], axis=1)
        blended = lax.map(lambda triple: attend(triple[0], triple[1], triple[2], QLEN), (turned, key_rows, value_rows))
        return jnp.transpose(blended.reshape(HEADS, QLEN, HD), (1, 0, 2)).reshape(QLEN, HEADS * HD)
    attention = lax.map(one_request, (queries.reshape(REQUESTS, QLEN, HEADS, HD), question_kv.reshape(REQUESTS, QLEN, KV_HEADS, 2, HD), passage_ids, slot_offsets))
    attention = attention.reshape(REQUESTS * QLEN, HEADS * HD).astype(jnp.bfloat16)
    projected = jnp.dot(attention, out_weight, preferred_element_type=jnp.float32)
    question_out = (question_states.astype(jnp.float32) + projected).astype(jnp.bfloat16)
    return (passage_kv, question_out)
```

```python
import math

import jax
import jax.numpy as jnp
from jax import lax
from jax.sharding import PartitionSpec as P

D = 8192
KV_HEADS = 8
HD = 128
PLEN = 256
QLEN = 128
SIDE = 2


def rope_tables(positions):
    half_dim = HD // 2
    inverse = jnp.exp(
        jnp.arange(half_dim, dtype=jnp.float32) * (-2.0 * math.log(500000.0) / HD)
    )
    angles = positions.astype(jnp.float32)[:, None] * inverse[None, :]
    return jnp.cos(angles), jnp.sin(angles)


def rotate(matrix, tables):
    cosine, sine_part = tables
    half_dim = matrix.shape[-1] // 2
    first_half = matrix[..., :half_dim]
    second = matrix[..., half_dim:]
    return jnp.concatenate(
        [first_half * cosine - second * sine_part, second * cosine + first_half * sine_part],
        axis=-1,
    )


def attend(turned, key_rows, value_rows, question_len):
    scores = lax.dot_general(
        turned, key_rows, (((1,), (1,)), ((), ())), preferred_element_type=jnp.float32
    )
    key_count = key_rows.shape[0]
    cached = key_count - question_len
    row_pos = jnp.arange(turned.shape[0], dtype=jnp.int32) % question_len
    col_pos = jnp.arange(key_count, dtype=jnp.int32)
    allowed = (col_pos[None, :] < cached) | (col_pos[None, :] - cached <= row_pos[:, None])
    scores = jnp.where(allowed, scores, -1e30)
    row_max = jnp.max(scores, axis=1, keepdims=True)
    weights = jnp.where(allowed, jnp.exp(scores - row_max), 0.0)
    total_weight = jnp.sum(weights, axis=1, keepdims=True)
    blended = jnp.dot(weights.astype(jnp.bfloat16), value_rows, preferred_element_type=jnp.float32)
    return blended / total_weight


def one_request(request_q, request_kv, chosen, offsets, stored):
    question_len = request_q.shape[0]
    head_dim = request_kv.shape[1] // 2
    heads_here = request_q.shape[1] // head_dim
    passage_len = stored.shape[1]
    slot_count = chosen.shape[0]
    q_pos = slot_count * passage_len + jnp.arange(question_len, dtype=jnp.int32)
    q_tables = rope_tables(q_pos)
    turned = rotate(
        jnp.transpose(request_q.reshape(question_len, heads_here, head_dim), (1, 0, 2)), q_tables
    ) * HD ** (-0.5)
    turned = turned.astype(jnp.bfloat16).reshape(heads_here * question_len, head_dim)
    picked = stored[chosen].reshape(slot_count * passage_len, 2 * head_dim)
    p_pos = (offsets[:, None] + jnp.arange(passage_len, dtype=jnp.int32)[None, :]).reshape(
        slot_count * passage_len
    )
    key_rows = jnp.concatenate(
        [
            rotate(picked[:, :head_dim].astype(jnp.float32), rope_tables(p_pos)),
            rotate(request_kv[:, :head_dim].astype(jnp.float32), q_tables),
        ],
        axis=0,
    ).astype(jnp.bfloat16)
    value_rows = jnp.concatenate([picked[:, head_dim:], request_kv[:, head_dim:]], axis=0)
    blended = attend(turned, key_rows, value_rows, question_len)
    return jnp.transpose(blended.reshape(heads_here, question_len, head_dim), (1, 0, 2)).reshape(
        question_len, heads_here * head_dim
    )


def line_perms(n):
    depth = n // SIDE
    across = [(h, h ^ 1) for h in range(n)]
    return depth, across


def hop(value, n, senders, direction):
    perm = [
        (z * SIDE + y, (z + direction) * SIDE + y)
        for z in senders
        if 0 <= z + direction < n // SIDE
        for y in range(SIDE)
    ]
    return lax.ppermute(value, "head", perm)


def pick(index, choices):
    result = choices[0]
    left = [c for c in choices if c is not result]
    while left:
        array = left[0]
        mask = False
        for i, choice in enumerate(choices):
            if choice is array:
                mask = mask | (index == i)
        result = jnp.where(mask, array, result)
        left = [c for c in left if c is not array]
    return result


def table_at(index, values):
    return jnp.asarray(values, jnp.int32)[index]


def all_sum_small(values, n):
    step = 1
    while step < n:
        values = values + lax.ppermute(values, "head", [(h, h ^ step) for h in range(n)])
        step *= 2
    return values


def gather_parts(part, n):
    depth, across = line_perms(n)
    me = lax.axis_index("head")
    z, y = me // SIDE, me % SIDE
    other = 1 - y
    ups, downs = [part], [part]
    out = [(part, me)]
    order = []
    for zz in range(depth):
        near = []
        for s in range(1, depth):
            if zz - s >= 0:
                near.append((s, True))
            if zz + s < depth:
                near.append((s, False))
        order.append(near)
    crossing = [lax.ppermute(part, "head", across)]
    out.append((crossing[0], z * SIDE + other))
    for s in range(1, depth):
        ups.append(hop(ups[-1], n, range(s - 1, depth), 1))
        downs.append(hop(downs[-1], n, range(depth - s + 1), -1))
        slot = [order[zz][s - 1] for zz in range(depth)]
        came = pick(z, [(ups if u else downs)[d] for d, u in slot])
        source = table_at(z, [zz - d if u else zz + d for zz, (d, u) in enumerate(slot)])
        out.append((came, source * SIDE + y))
        out.append((lax.ppermute(came, "head", across), source * SIDE + other))
    return out


def scatter_sum_line_first(block_of, n):
    depth, across = line_perms(n)
    me = lax.axis_index("head")
    z, y = me // SIDE, me % SIDE
    came_up = came_down = None
    for k in range(depth - 1, 0, -1):
        send_up = block_of(jnp.minimum(z + k, depth - 1))
        send_down = block_of(jnp.maximum(z - k, 0))
        if came_up is not None:
            send_up = send_up + came_up.astype(jnp.float32)
            send_down = send_down + came_down.astype(jnp.float32)
        came_up = hop(send_up.astype(jnp.bfloat16), n, range(depth - k), 1)
        came_down = hop(send_down.astype(jnp.bfloat16), n, range(k, depth), -1)
    total = block_of(z) + came_up.astype(jnp.float32) + came_down.astype(jnp.float32)
    first, second = jnp.split(total, 2, axis=1)
    keep = jnp.where(y == 0, first, second)
    give = jnp.where(y == 0, second, first).astype(jnp.bfloat16)
    return keep + lax.ppermute(give, "head", across).astype(jnp.float32)


def scatter_sum_side_first(block_of, n):
    depth, across = line_perms(n)
    me = lax.axis_index("head")
    z, y = me // SIDE, me % SIDE
    order = [sorted(range(depth), key=lambda d, zz=zz: (-abs(d - zz), d)) for zz in range(depth)]
    pairs = []

    def cross(slot):
        dest = table_at(z, [order[zz][slot] for zz in range(depth)]) * SIDE
        came = lax.ppermute(block_of(dest + 1 - y).astype(jnp.bfloat16), "head", across)
        pairs.append(came.astype(jnp.float32) + block_of(dest + y))

    def pair_sum(offset):
        chosen = []
        for zz in range(depth):
            d = min(max(zz + offset, 0), depth - 1)
            slot = order[zz].index(d)
            chosen.append(pairs[slot] if zz + offset == d else None)
        known = [c for c in chosen if c is not None]
        return pick(z, [known[0] if c is None else c for c in chosen])

    came_up = came_down = None
    for step in range(depth - 1):
        k = depth - 1 - step
        cross(step)
        send_up, send_down = pair_sum(k), pair_sum(-k)
        if came_up is not None:
            send_up = send_up + came_up.astype(jnp.float32)
            send_down = send_down + came_down.astype(jnp.float32)
        came_up = hop(send_up.astype(jnp.bfloat16), n, range(depth - k), 1)
        came_down = hop(send_down.astype(jnp.bfloat16), n, range(k, depth), -1)
    cross(depth - 1)
    return pair_sum(0) + came_up.astype(jnp.float32) + came_down.astype(jnp.float32)


def spread_heads(matrix, group_size):
    if group_size == 1:
        return matrix
    leading = matrix.shape[0]
    per_head = matrix.reshape(leading, KV_HEADS, 2 * HD)
    return jnp.repeat(per_head, group_size, axis=1).reshape(leading, KV_HEADS * group_size * 2 * HD)


def local(
    passage_states,
    question_states,
    norm_gain,
    query_weight,
    kv_weight,
    out_weight,
    passage_ids,
    slot_offsets,
):
    n = lax.axis_size("head")
    items = lax.axis_size("item")
    pas_rows = passage_states.shape[0]
    question_rows = question_states.shape[0]
    features = norm_gain.shape[0]
    group_size = n // KV_HEADS
    block_cols = kv_weight.shape[1] // n
    query_cols = query_weight.shape[1]

    def normed(states):
        rows = states.astype(jnp.float32)
        return (rows * norm_gain[None, :]).astype(jnp.bfloat16), jnp.sum(rows * rows, axis=1)

    gained_q, squares_q = normed(question_states)
    gained_p, squares_p = normed(passage_states)
    squares = all_sum_small(jnp.concatenate([squares_p, squares_q]), n)
    row_scale = lax.rsqrt(squares / D + 1e-05)[:, None]

    parts = gather_parts(gained_q, n)

    gained = jnp.concatenate([gained_p, gained_q], axis=0)
    kv_partial = jnp.dot(
        gained, spread_heads(kv_weight, group_size), preferred_element_type=jnp.float32
    )
    pair_cols = SIDE * 2 * HD
    kv_sums = scatter_sum_line_first(
        lambda zz: lax.dynamic_slice_in_dim(kv_partial, zz * pair_cols, pair_cols, 1), n
    )
    kv_head = (row_scale * kv_sums).astype(jnp.bfloat16)
    own_start = lax.axis_index("head") % group_size * block_cols
    passage_out = lax.dynamic_slice_in_dim(kv_head[:pas_rows], own_start, block_cols, 1)

    query_sums = jnp.zeros((question_rows, query_cols), jnp.float32)
    for part, owner in parts:
        rows = lax.dynamic_slice_in_dim(query_weight, owner * features, features, 0)
        query_sums = query_sums + jnp.dot(part, rows, preferred_element_type=jnp.float32)
    queries = row_scale[pas_rows:] * query_sums

    stored = lax.all_gather(kv_head[:pas_rows], "item", axis=0, tiled=True)
    stored = stored.reshape(stored.shape[0] // PLEN, PLEN, stored.shape[1])
    request_count = question_rows // QLEN
    blended = jax.vmap(one_request, in_axes=(0, 0, 0, 0, None))(
        queries.reshape(request_count, QLEN, query_cols),
        kv_head[pas_rows:].reshape(request_count, QLEN, kv_head.shape[1]),
        passage_ids,
        slot_offsets,
        stored,
    )
    attention = blended.reshape(question_rows, query_cols).astype(jnp.bfloat16)

    def out_block(device):
        columns = lax.dynamic_slice_in_dim(out_weight, device * features, features, 1)
        return jnp.dot(attention, columns, preferred_element_type=jnp.float32)

    summed = scatter_sum_side_first(out_block, n)
    question_out = (question_states.astype(jnp.float32) + summed).astype(jnp.bfloat16)
    return (passage_out, question_out)


def solution(mesh):
    return jax.shard_map(
        local,
        mesh=mesh,
        in_specs=(
            P(("grp", "item"), "head"),
            P(("grp", "item"), "head"),
            P("head"),
            P(None, "head"),
            P("head", None),
            P("head", None),
            P(("grp", "item"), None),
            P(("grp", "item"), None),
        ),
        out_specs=(P(("grp", "item"), "head"), P(("grp", "item"), "head")),
        check_vma=False,
    )
```

```python
import math

import jax
import jax.numpy as jnp
from jax import lax
from jax.sharding import PartitionSpec as P

D = 8192
KV_HEADS = 8
HD = 128
PLEN = 256
QLEN = 128
SIDE = 2


def rope_tables(positions):
    half_dim = HD // 2
    inverse = jnp.exp(
        jnp.arange(half_dim, dtype=jnp.float32) * (-2.0 * math.log(500000.0) / HD)
    )
    angles = positions.astype(jnp.float32)[:, None] * inverse[None, :]
    return jnp.cos(angles), jnp.sin(angles)


def rotate(matrix, tables):
    cosine, sine_part = tables
    half_dim = matrix.shape[-1] // 2
    first_half = matrix[..., :half_dim]
    second = matrix[..., half_dim:]
    return jnp.concatenate(
        [first_half * cosine - second * sine_part, second * cosine + first_half * sine_part],
        axis=-1,
    )


def attend(turned, key_rows, value_rows, question_len):
    scores = lax.dot_general(
        turned, key_rows, (((1,), (1,)), ((), ())), preferred_element_type=jnp.float32
    )
    key_count = key_rows.shape[0]
    cached = key_count - question_len
    row_pos = jnp.arange(turned.shape[0], dtype=jnp.int32) % question_len
    col_pos = jnp.arange(key_count, dtype=jnp.int32)
    allowed = (col_pos[None, :] < cached) | (col_pos[None, :] - cached <= row_pos[:, None])
    scores = jnp.where(allowed, scores, -1e30)
    row_max = jnp.max(scores, axis=1, keepdims=True)
    weights = jnp.where(allowed, jnp.exp(scores - row_max), 0.0)
    total_weight = jnp.sum(weights, axis=1, keepdims=True)
    blended = jnp.dot(weights.astype(jnp.bfloat16), value_rows, preferred_element_type=jnp.float32)
    return blended / total_weight


def one_request(request_q, request_kv, chosen, offsets, stored):
    question_len = request_q.shape[0]
    head_dim = request_kv.shape[1] // 2
    heads_here = request_q.shape[1] // head_dim
    passage_len = stored.shape[1]
    slot_count = chosen.shape[0]
    q_pos = slot_count * passage_len + jnp.arange(question_len, dtype=jnp.int32)
    q_tables = rope_tables(q_pos)
    turned = rotate(
        jnp.transpose(request_q.reshape(question_len, heads_here, head_dim), (1, 0, 2)), q_tables
    ) * HD ** (-0.5)
    turned = turned.astype(jnp.bfloat16).reshape(heads_here * question_len, head_dim)
    picked = stored[chosen].reshape(slot_count * passage_len, 2 * head_dim)
    p_pos = (offsets[:, None] + jnp.arange(passage_len, dtype=jnp.int32)[None, :]).reshape(
        slot_count * passage_len
    )
    key_rows = jnp.concatenate(
        [
            rotate(picked[:, :head_dim].astype(jnp.float32), rope_tables(p_pos)),
            rotate(request_kv[:, :head_dim].astype(jnp.float32), q_tables),
        ],
        axis=0,
    ).astype(jnp.bfloat16)
    value_rows = jnp.concatenate([picked[:, head_dim:], request_kv[:, head_dim:]], axis=0)
    blended = attend(turned, key_rows, value_rows, question_len)
    return jnp.transpose(blended.reshape(heads_here, question_len, head_dim), (1, 0, 2)).reshape(
        question_len, heads_here * head_dim
    )


def line_perms(n):
    depth = n // SIDE
    across = [(h, h ^ 1) for h in range(n)]
    return depth, across


def hop(value, n, senders, direction):
    perm = [
        (z * SIDE + y, (z + direction) * SIDE + y)
        for z in senders
        if 0 <= z + direction < n // SIDE
        for y in range(SIDE)
    ]
    return lax.ppermute(value, "head", perm)


def pick(index, choices):
    result = choices[0]
    left = [c for c in choices if c is not result]
    while left:
        array = left[0]
        mask = False
        for i, choice in enumerate(choices):
            if choice is array:
                mask = mask | (index == i)
        result = jnp.where(mask, array, result)
        left = [c for c in left if c is not array]
    return result


def table_at(index, values):
    return jnp.asarray(values, jnp.int32)[index]


def orders(depth):
    return [sorted(range(depth), key=lambda d, z=z: (-abs(d - z), d)) for z in range(depth)]


def run(processes):
    results = [None] * len(processes)
    answers = [None] * len(processes)
    live = set(range(len(processes)))
    turn = 0
    while live:
        asked = {}
        for i, (start, process) in enumerate(processes):
            if i not in live or start > turn:
                continue
            try:
                asked[i] = process.send(answers[i])
            except StopIteration as stop:
                results[i] = stop.value
                live.discard(i)
        tied = {i: ([array for array, _ in sends], keeps) for i, (sends, keeps) in asked.items()}
        tied = lax.optimization_barrier(tied)
        for i, (sends, _) in asked.items():
            arrays, keeps = tied[i]
            answers[i] = ([move(array) for array, (_, move) in zip(arrays, sends)], keeps)
        turn += 1
    return results


def small_sum(values, n):
    step = 1
    while step < n:
        perm = [(h, h ^ step) for h in range(n)]
        (came,), (values,) = yield [(values, lambda v, perm=perm: lax.ppermute(v, "head", perm))], [values]
        values = values + came
        step *= 2
    return values


def gather_product(part, weight, n):
    depth, across = line_perms(n)
    features = part.shape[1]
    me = lax.axis_index("head")
    z, y = me // SIDE, me % SIDE
    other = 1 - y
    cross = lambda v: lax.ppermute(v, "head", across)
    order = []
    for zz in range(depth):
        near = []
        for s in range(1, depth):
            if zz - s >= 0:
                near.append((s, True))
            if zz + s < depth:
                near.append((s, False))
        order.append(near)

    def product(total, news):
        for came, owner in news:
            rows = lax.dynamic_slice_in_dim(weight, owner * features, features, 0)
            term = jnp.dot(came, rows, preferred_element_type=jnp.float32)
            total = term if total is None else total + term
        return total

    ups, downs = [part], [part]
    total, news, crossing = None, [(part, me)], (part, z)
    for s in range(1, depth + 1):
        sends = [(crossing[0], cross)]
        if s < depth:
            sends.append((ups[-1], lambda v, s=s: hop(v, n, range(s - 1, depth), 1)))
            sends.append((downs[-1], lambda v, s=s: hop(v, n, range(depth - s + 1), -1)))
        owners = [owner for _, owner in news]
        keeps = [[came for came, _ in news]] + ([] if total is None else [total])
        received, keeps = yield sends, keeps
        total = product(keeps[1] if len(keeps) > 1 else None, list(zip(keeps[0], owners)))
        news = [(received[0], crossing[1] * SIDE + other)]
        if s < depth:
            ups.append(received[1])
            downs.append(received[2])
            slot = [order[zz][s - 1] for zz in range(depth)]
            came = pick(z, [(ups if u else downs)[d] for d, u in slot])
            source = table_at(z, [zz - d if u else zz + d for zz, (d, u) in enumerate(slot)])
            crossing = (came, source)
            news.append((came, source * SIDE + y))
    return product(total, news)


def at_offset(z, depth, slots, offset):
    order = orders(depth)
    chosen = [
        slots[order[zz].index(zz + offset)] if 0 <= zz + offset < depth else None
        for zz in range(depth)
    ]
    known = [c for c in chosen if c is not None]
    return pick(z, [known[0] if c is None else c for c in chosen])


def at_distance(z, depth, slots, k):
    order = orders(depth)
    chosen = []
    for zz in range(depth):
        dest = zz + k if zz + k < depth else zz - k
        chosen.append(slots[order[zz].index(dest)] if 0 <= dest < depth else None)
    known = [c for c in chosen if c is not None]
    return pick(z, [known[0] if c is None else c for c in chosen])


def line_sends(z, n, slots, k, came):
    depth = n // SIDE
    up = lambda v: hop(v, n, range(depth - k), 1)
    down = lambda v: hop(v, n, range(k, depth), -1)
    if 2 * k > depth - 1:
        value = at_distance(z, depth, slots, k)
        for array in came:
            value = value + array.astype(jnp.float32)
        value = value.astype(jnp.bfloat16)
        return [(value, up), (value, down)]
    sends = []
    for i, move in enumerate((up, down)):
        value = at_offset(z, depth, slots, -k if i else k)
        if came:
            value = value + came[i].astype(jnp.float32)
        sends.append((value.astype(jnp.bfloat16), move))
    return sends


def scatter_line_first(block_of, source, n):
    depth, across = line_perms(n)
    me = lax.axis_index("head")
    z, y = me // SIDE, me % SIDE
    order = orders(depth)
    dest = [table_at(z, [order[zz][slot] for zz in range(depth)]) for slot in range(depth)]
    slots, came = [block_of(source, dest[0])], []
    if depth > 2:
        slots.append(block_of(source, dest[1]))
    for k in range(depth - 1, 0, -1):
        received, (source, slots) = yield line_sends(z, n, slots, k, came), [source, slots]
        came = received
        while len(slots) < min(depth, depth - k + 2):
            slots = slots + [block_of(source, dest[len(slots)])]
    total = slots[depth - 1] + came[0].astype(jnp.float32) + came[1].astype(jnp.float32)
    first, second = jnp.split(total, 2, axis=1)
    keep = jnp.where(y == 0, first, second)
    give = jnp.where(y == 0, second, first).astype(jnp.bfloat16)
    received, (keep,) = yield [(give, lambda v: lax.ppermute(v, "head", across))], [keep]
    return keep + received[0].astype(jnp.float32)


def scatter_side_first(block_of, source, n):
    depth, across = line_perms(n)
    me = lax.axis_index("head")
    z, y = me // SIDE, me % SIDE
    order = orders(depth)
    cross = lambda v: lax.ppermute(v, "head", across)
    dest = [
        table_at(z, [order[zz][slot] for zz in range(depth)]) * SIDE for slot in range(depth)
    ]
    slots, came = [], []
    give = block_of(source, dest[0] + 1 - y).astype(jnp.bfloat16)
    for turn in range(depth):
        sends = [(give, cross)]
        if turn:
            sends += line_sends(z, n, slots, depth - turn, came)
        received, (source, slots) = yield sends, [source, slots]
        came = received[1:]
        if turn + 1 < depth:
            give = block_of(source, dest[turn + 1] + 1 - y).astype(jnp.bfloat16)
        mine = block_of(source, dest[turn] + y)
        slots = slots + [mine + received[0].astype(jnp.float32)]
    total = slots[depth - 1]
    for array in came:
        total = total + array.astype(jnp.float32)
    return total


def spread_heads(matrix, group_size):
    if group_size == 1:
        return matrix
    leading = matrix.shape[0]
    per_head = matrix.reshape(leading, KV_HEADS, 2 * HD)
    return jnp.repeat(per_head, group_size, axis=1).reshape(leading, KV_HEADS * group_size * 2 * HD)


def local(
    passage_states,
    question_states,
    norm_gain,
    query_weight,
    kv_weight,
    out_weight,
    passage_ids,
    slot_offsets,
):
    n = lax.axis_size("head")
    pas_rows = passage_states.shape[0]
    question_rows = question_states.shape[0]
    features = norm_gain.shape[0]
    group_size = n // KV_HEADS
    block_cols = kv_weight.shape[1] // n
    query_cols = query_weight.shape[1]

    def normed(states):
        rows = states.astype(jnp.float32)
        return (rows * norm_gain[None, :]).astype(jnp.bfloat16), jnp.sum(rows * rows, axis=1)

    gained_q, squares_q = normed(question_states)
    gained_p, squares_p = normed(passage_states)
    spread = spread_heads(kv_weight, group_size)

    def kv_columns(cols):
        def block_of(rows, index):
            weight = lax.dynamic_slice_in_dim(spread, index * cols, cols, 1)
            return jnp.dot(rows, weight, preferred_element_type=jnp.float32)

        return block_of

    query_sums, squares, passage_sums, request_sums = run(
        [
            (0, gather_product(gained_q, query_weight, n)),
            (1, small_sum(jnp.concatenate([squares_p, squares_q]), n)),
            (1, scatter_line_first(kv_columns(SIDE * 2 * HD), gained_p, n)),
            (1, scatter_side_first(kv_columns(2 * HD), gained_q, n)),
        ]
    )
    row_scale = lax.rsqrt(squares / D + 1e-05)[:, None]
    passage_kv = (row_scale[:pas_rows] * passage_sums).astype(jnp.bfloat16)
    request_kv = (row_scale[pas_rows:] * request_sums).astype(jnp.bfloat16)
    own_start = lax.axis_index("head") % group_size * block_cols
    passage_out = lax.dynamic_slice_in_dim(passage_kv, own_start, block_cols, 1)
    queries = row_scale[pas_rows:] * query_sums

    stored = lax.all_gather(passage_kv, "item", axis=0, tiled=True)
    stored = stored.reshape(stored.shape[0] // PLEN, PLEN, stored.shape[1])
    request_count = question_rows // QLEN
    blended = jax.vmap(one_request, in_axes=(0, 0, 0, 0, None))(
        queries.reshape(request_count, QLEN, query_cols),
        request_kv.reshape(request_count, QLEN, request_kv.shape[1]),
        passage_ids,
        slot_offsets,
        stored,
    )
    attention = blended.reshape(question_rows, query_cols).astype(jnp.bfloat16)

    def out_block(rows, device):
        columns = lax.dynamic_slice_in_dim(out_weight, device * features, features, 1)
        return jnp.dot(rows, columns, preferred_element_type=jnp.float32)

    (summed,) = run([(0, scatter_side_first(out_block, attention, n))])
    question_out = (question_states.astype(jnp.float32) + summed).astype(jnp.bfloat16)
    return (passage_out, question_out)


def solution(mesh):
    return jax.shard_map(
        local,
        mesh=mesh,
        in_specs=(
            P(("grp", "item"), "head"),
            P(("grp", "item"), "head"),
            P("head"),
            P(None, "head"),
            P("head", None),
            P("head", None),
            P(("grp", "item"), None),
            P(("grp", "item"), None),
        ),
        out_specs=(P(("grp", "item"), "head"), P(("grp", "item"), "head")),
        check_vma=False,
    )
```

```python
import math

import jax
import jax.numpy as jnp
from jax import lax
from jax.sharding import PartitionSpec as P

D = 8192
KV_HEADS = 8
HD = 128
PLEN = 256
QLEN = 128
SIDE = 2


def rope_tables(positions):
    half_dim = HD // 2
    inverse = jnp.exp(
        jnp.arange(half_dim, dtype=jnp.float32) * (-2.0 * math.log(500000.0) / HD)
    )
    angles = positions.astype(jnp.float32)[:, None] * inverse[None, :]
    return jnp.cos(angles), jnp.sin(angles)


def rotate(matrix, tables):
    cosine, sine_part = tables
    half_dim = matrix.shape[-1] // 2
    first_half = matrix[..., :half_dim]
    second = matrix[..., half_dim:]
    return jnp.concatenate(
        [first_half * cosine - second * sine_part, second * cosine + first_half * sine_part],
        axis=-1,
    )


def attend(turned, key_rows, value_rows, question_len):
    scores = lax.dot_general(
        turned, key_rows, (((1,), (1,)), ((), ())), preferred_element_type=jnp.float32
    )
    key_count = key_rows.shape[0]
    cached = key_count - question_len
    row_pos = jnp.arange(turned.shape[0], dtype=jnp.int32) % question_len
    col_pos = jnp.arange(key_count, dtype=jnp.int32)
    allowed = (col_pos[None, :] < cached) | (col_pos[None, :] - cached <= row_pos[:, None])
    scores = jnp.where(allowed, scores, -1e30)
    row_max = jnp.max(scores, axis=1, keepdims=True)
    weights = jnp.where(allowed, jnp.exp(scores - row_max), 0.0)
    total_weight = jnp.sum(weights, axis=1, keepdims=True)
    blended = jnp.dot(weights.astype(jnp.bfloat16), value_rows, preferred_element_type=jnp.float32)
    return blended / total_weight


def one_request(request_q, request_kv, chosen, offsets, stored):
    question_len = request_q.shape[0]
    head_dim = request_kv.shape[1] // 2
    heads_here = request_q.shape[1] // head_dim
    passage_len = stored.shape[1]
    slot_count = chosen.shape[0]
    q_pos = slot_count * passage_len + jnp.arange(question_len, dtype=jnp.int32)
    q_tables = rope_tables(q_pos)
    turned = rotate(
        jnp.transpose(request_q.reshape(question_len, heads_here, head_dim), (1, 0, 2)), q_tables
    ) * HD ** (-0.5)
    turned = turned.astype(jnp.bfloat16).reshape(heads_here * question_len, head_dim)
    picked = stored[chosen].reshape(slot_count * passage_len, 2 * head_dim)
    p_pos = (offsets[:, None] + jnp.arange(passage_len, dtype=jnp.int32)[None, :]).reshape(
        slot_count * passage_len
    )
    key_rows = jnp.concatenate(
        [
            rotate(picked[:, :head_dim].astype(jnp.float32), rope_tables(p_pos)),
            rotate(request_kv[:, :head_dim].astype(jnp.float32), q_tables),
        ],
        axis=0,
    ).astype(jnp.bfloat16)
    value_rows = jnp.concatenate([picked[:, head_dim:], request_kv[:, head_dim:]], axis=0)
    blended = attend(turned, key_rows, value_rows, question_len)
    return jnp.transpose(blended.reshape(heads_here, question_len, head_dim), (1, 0, 2)).reshape(
        question_len, heads_here * head_dim
    )


def line_perms(n):
    depth = n // SIDE
    across = [(h, h ^ 1) for h in range(n)]
    return depth, across


def hop(value, n, senders, direction):
    perm = [
        (z * SIDE + y, (z + direction) * SIDE + y)
        for z in senders
        if 0 <= z + direction < n // SIDE
        for y in range(SIDE)
    ]
    return lax.ppermute(value, "head", perm)


def pick(index, choices):
    result = choices[0]
    left = [c for c in choices if c is not result]
    while left:
        array = left[0]
        mask = False
        for i, choice in enumerate(choices):
            if choice is array:
                mask = mask | (index == i)
        result = jnp.where(mask, array, result)
        left = [c for c in left if c is not array]
    return result


def table_at(index, values):
    return jnp.asarray(values, jnp.int32)[index]


def orders(depth):
    return [sorted(range(depth), key=lambda d, z=z: (-abs(d - z), d)) for z in range(depth)]


def tie(*trees):
    return lax.optimization_barrier(trees)


def fold(rows, height):
    if rows.shape[0] == height:
        return rows
    return jnp.concatenate(jnp.split(rows, rows.shape[0] // height, axis=0), axis=1)


def unfold(block, cols):
    if block.shape[1] == cols:
        return block
    return jnp.concatenate(jnp.split(block, block.shape[1] // cols, axis=1), axis=0)


def widen(array, cols):
    if array.shape[1] == cols:
        return array
    return jnp.pad(array, ((0, 0), (0, cols - array.shape[1])))


def join(arrays):
    return arrays[0] if len(arrays) == 1 else jnp.concatenate(arrays, axis=1)


def at_offset(z, depth, slots, offset):
    order = orders(depth)
    chosen = [
        slots[order[zz].index(zz + offset)] if 0 <= zz + offset < depth else None
        for zz in range(depth)
    ]
    known = [c for c in chosen if c is not None]
    return pick(z, [known[0] if c is None else c for c in chosen])


def at_distance(z, depth, slots, k):
    order = orders(depth)
    chosen = []
    for zz in range(depth):
        dest = zz + k if zz + k < depth else zz - k
        chosen.append(slots[order[zz].index(dest)] if 0 <= dest < depth else None)
    known = [c for c in chosen if c is not None]
    return pick(z, [known[0] if c is None else c for c in chosen])


def line_values(z, n, slots, k, came):
    depth = n // SIDE
    if 2 * k > depth - 1:
        value = at_distance(z, depth, slots, k)
        if came:
            value = value + jnp.where(z < depth - k, *came).astype(jnp.float32)
        value = value.astype(jnp.bfloat16)
        return value, value
    values = []
    for i in range(2):
        value = at_offset(z, depth, slots, -k if i else k)
        if came:
            value = value + came[i].astype(jnp.float32)
        values.append(value.astype(jnp.bfloat16))
    return tuple(values)


def project(part, passages, query_weight, kv_weight, n):
    depth, across = line_perms(n)
    features = part.shape[1]
    height = part.shape[0]
    cols = 2 * HD
    me = lax.axis_index("head")
    z, y = me // SIDE, me % SIDE
    other = 1 - y
    order = orders(depth)
    dest = [table_at(z, [order[zz][slot] for zz in range(depth)]) for slot in range(depth)]
    width = max(features, passages.shape[0] // height * SIDE * cols)
    arrivals = []
    for zz in range(depth):
        near = []
        for s in range(1, depth):
            if zz - s >= 0:
                near.append((s, True))
            if zz + s < depth:
                near.append((s, False))
        arrivals.append(near)

    def product(total, news):
        for came, owner in news:
            rows = lax.dynamic_slice_in_dim(query_weight, owner * features, features, 0)
            term = jnp.dot(came, rows, preferred_element_type=jnp.float32)
            total = term if total is None else total + term
        return total

    def kv_product(rows, start, count):
        weight = lax.dynamic_slice_in_dim(kv_weight, start, count, 1)
        return jnp.dot(rows, weight, preferred_element_type=jnp.float32)

    ups, downs, crossing = [part], [part], (part, z)
    total, news = None, [(part, me)]
    p_slots, p_came = [], ()
    q_slots, q_came, q_give = [], (), None
    questions = part
    for t in range(1, depth + 2):
        to_y = []
        to_z = ([], [])
        if t <= depth:
            to_y.append(crossing[0])
        if t == 1:
            for side in to_z:
                side.append(widen(part, width))
        elif t <= depth:
            values = line_values(z, n, p_slots, depth - t + 1, p_came)
            gathered = (ups[-1], downs[-1])
            for i, place in enumerate((z, depth - 1 - z)):
                mine = widen(fold(values[i], height), width)
                to_z[i].append(jnp.where(place < t - 1, mine, widen(gathered[i], width)))
        else:
            p_total = p_slots[depth - 1]
            for array in p_came:
                p_total = p_total + array.astype(jnp.float32)
            first, second = jnp.split(p_total, 2, axis=1)
            p_keep = jnp.where(y == 0, first, second)
            to_y.append(fold(jnp.where(y == 0, second, first).astype(jnp.bfloat16), height))
        if t >= 2:
            to_y.append(q_give)
        if t >= 3:
            for side, value in zip(to_z, line_values(z, n, q_slots, depth - t + 2, q_came)):
                side.append(value)
        sends, news_arrays, total, passages, questions, p_slots, q_slots = tie(
            [join(to_y), join(to_z[0]), join(to_z[1])],
            [came for came, _ in news],
            [] if total is None else [total],
            passages,
            questions,
            p_slots,
            q_slots,
        )
        last = t > depth
        received = [
            lax.ppermute(sends[0], "head", across),
            hop(sends[1], n, range(depth), 1),
            hop(sends[2], n, range(depth), -1),
        ]
        total = product(total[0] if total else None, [(c, o) for c, (_, o) in zip(news_arrays, news)])
        new_p = [kv_product(passages, dest[t - 1] * SIDE * cols, SIDE * cols)] if t <= depth else []
        q_mine = []
        if t >= 2:
            q_mine = [kv_product(questions, (dest[t - 2] * SIDE + y) * cols, cols)]
        new_give = []
        if t <= depth:
            new_give = [
                kv_product(questions, (dest[t - 1] * SIDE + other) * cols, cols).astype(jnp.bfloat16)
            ]
        received, total, new_p, q_mine, new_give = tie(received, total, new_p, q_mine, new_give)
        p_slots = p_slots + new_p
        q_give = new_give[0] if new_give else None
        taken = 0
        news = []
        if t <= depth:
            news.append((received[0][:, :features], crossing[1] * SIDE + other))
            taken = features
        else:
            taken = passages.shape[0] // height * cols
            p_came_y = unfold(received[0][:, :taken], cols)
        if t >= 2:
            q_slots = q_slots + [q_mine[0] + received[0][:, taken:].astype(jnp.float32)]
        if t < depth:
            ups.append(received[1][:, :features])
            downs.append(received[2][:, :features])
            slot = [arrivals[zz][t - 1] for zz in range(depth)]
            came = pick(z, [(ups if u else downs)[d] for d, u in slot])
            source = table_at(z, [zz - d if u else zz + d for zz, (d, u) in enumerate(slot)])
            crossing = (came, source)
            news.append((came, source * SIDE + y))
        if 2 <= t <= depth:
            used = passages.shape[0] // height * SIDE * cols
            p_came = tuple(unfold(r[:, :used], SIDE * cols) for r in received[1:])
        if t >= 3:
            q_came = tuple(r[:, (0 if last else width) :] for r in received[1:])
    q_total = q_slots[depth - 1]
    for array in q_came:
        q_total = q_total + array.astype(jnp.float32)
    return product(total, news), p_keep + p_came_y.astype(jnp.float32), q_total


def scatter_sum(block_of, source, n):
    depth, across = line_perms(n)
    me = lax.axis_index("head")
    z, y = me // SIDE, me % SIDE
    order = orders(depth)
    dest = [
        table_at(z, [order[zz][slot] for zz in range(depth)]) * SIDE for slot in range(depth)
    ]
    slots, came = [], []
    give = block_of(source, dest[0] + 1 - y).astype(jnp.bfloat16)
    for turn in range(depth):
        sends = [give]
        if turn:
            sends += line_values(z, n, slots, depth - turn, came)
        sends, source, slots = tie(sends, source, slots)
        received = [lax.ppermute(sends[0], "head", across)]
        if turn:
            received.append(hop(sends[1], n, range(turn), 1))
            received.append(hop(sends[2], n, range(depth - turn, depth), -1))
        mine = block_of(source, dest[turn] + y)
        gives = []
        if turn + 1 < depth:
            gives = [block_of(source, dest[turn + 1] + 1 - y).astype(jnp.bfloat16)]
        received, mine, gives = tie(received, mine, gives)
        give = gives[0] if gives else None
        came = received[1:]
        slots = slots + [mine + received[0].astype(jnp.float32)]
    total = slots[depth - 1]
    for array in came:
        total = total + array.astype(jnp.float32)
    return total


def spread_heads(matrix, group_size):
    if group_size == 1:
        return matrix
    leading = matrix.shape[0]
    per_head = matrix.reshape(leading, KV_HEADS, 2 * HD)
    return jnp.repeat(per_head, group_size, axis=1).reshape(leading, KV_HEADS * group_size * 2 * HD)


def local(
    passage_states,
    question_states,
    norm_gain,
    query_weight,
    kv_weight,
    out_weight,
    passage_ids,
    slot_offsets,
):
    n = lax.axis_size("head")
    pas_rows = passage_states.shape[0]
    question_rows = question_states.shape[0]
    features = norm_gain.shape[0]
    group_size = n // KV_HEADS
    block_cols = kv_weight.shape[1] // n
    query_cols = query_weight.shape[1]

    def normed(states):
        rows = states.astype(jnp.float32)
        return (rows * norm_gain[None, :]).astype(jnp.bfloat16), jnp.sum(rows * rows, axis=1)

    gained_q, squares_q = normed(question_states)
    gained_p, squares_p = normed(passage_states)
    spread = spread_heads(kv_weight, group_size)

    squares = jnp.concatenate([squares_p, squares_q])
    squares = jnp.sum(lax.all_gather(squares, "head"), axis=0)
    query_sums, passage_sums, request_sums = project(gained_q, gained_p, query_weight, spread, n)
    row_scale = lax.rsqrt(squares / D + 1e-05)[:, None]
    passage_kv = (row_scale[:pas_rows] * passage_sums).astype(jnp.bfloat16)
    request_kv = (row_scale[pas_rows:] * request_sums).astype(jnp.bfloat16)
    own_start = lax.axis_index("head") % group_size * block_cols
    passage_out = lax.dynamic_slice_in_dim(passage_kv, own_start, block_cols, 1)
    queries = row_scale[pas_rows:] * query_sums

    stored = lax.all_gather(passage_kv, "item", axis=0, tiled=True)
    stored = stored.reshape(stored.shape[0] // PLEN, PLEN, stored.shape[1])
    request_count = question_rows // QLEN
    blended = jax.vmap(one_request, in_axes=(0, 0, 0, 0, None))(
        queries.reshape(request_count, QLEN, query_cols),
        request_kv.reshape(request_count, QLEN, request_kv.shape[1]),
        passage_ids,
        slot_offsets,
        stored,
    )
    attention = blended.reshape(question_rows, query_cols).astype(jnp.bfloat16)

    def out_block(rows, device):
        columns = lax.dynamic_slice_in_dim(out_weight, device * features, features, 1)
        return jnp.dot(rows, columns, preferred_element_type=jnp.float32)

    summed = scatter_sum(out_block, attention, n)
    question_out = (question_states.astype(jnp.float32) + summed).astype(jnp.bfloat16)
    return (passage_out, question_out)


def solution(mesh):
    return jax.shard_map(
        local,
        mesh=mesh,
        in_specs=(
            P(("grp", "item"), "head"),
            P(("grp", "item"), "head"),
            P("head"),
            P(None, "head"),
            P("head", None),
            P("head", None),
            P(("grp", "item"), None),
            P(("grp", "item"), None),
        ),
        out_specs=(P(("grp", "item"), "head"), P(("grp", "item"), "head")),
        check_vma=False,
    )
```

```python
import math

import jax
import jax.numpy as jnp
from jax import lax
from jax.experimental import pallas as pl
from jax.experimental.pallas import tpu as pltpu
from jax.sharding import PartitionSpec as P

D = 8192
KV_HEADS = 8
HD = 128
PLEN = 256
QLEN = 128
SIDE = 2


def rope_tables(positions):
    half_dim = HD // 2
    inverse = jnp.exp(
        jnp.arange(half_dim, dtype=jnp.float32) * (-2.0 * math.log(500000.0) / HD)
    )
    angles = positions.astype(jnp.float32)[:, None] * inverse[None, :]
    cosine, sine_part = jnp.cos(angles), jnp.sin(angles)
    return (
        jnp.concatenate([cosine, cosine], axis=1),
        jnp.concatenate([-sine_part, sine_part], axis=1),
    )


def attention_kernel(
    ids, offsets, sums, scale, request_kv, stored, cosines, sines, out, turned, keys, values
):
    request = pl.program_id(0)
    slots = ids.shape[1]
    cached = slots * PLEN
    total_keys = cached + QLEN
    heads = sums.shape[1] // HD

    def rot(vectors, cosine, sine):
        return vectors * cosine + pltpu.roll(vectors, HD // 2, 1) * sine

    q_cos = cosines[pl.ds(cached, QLEN), :]
    q_sin = sines[pl.ds(cached, QLEN), :]
    for slot in range(slots):
        start = pl.multiple_of(ids[request, slot] * PLEN, PLEN)
        offset = offsets[request, slot]
        rows = slice(slot * PLEN, (slot + 1) * PLEN)
        key = stored[pl.ds(start, PLEN), :HD].astype(jnp.float32)
        key = rot(key, cosines[pl.ds(offset, PLEN), :], sines[pl.ds(offset, PLEN), :])
        keys[rows, :] = key.astype(jnp.bfloat16)
        values[rows, :] = stored[pl.ds(start, PLEN), HD:]
    key = rot(request_kv[:, :HD].astype(jnp.float32), q_cos, q_sin)
    keys[cached:, :] = key.astype(jnp.bfloat16)
    values[cached:, :] = request_kv[:, HD:]
    row_scale = scale[...]
    for head in range(heads):
        query = row_scale * sums[:, head * HD : (head + 1) * HD]
        query = rot(query, q_cos, q_sin) * HD ** (-0.5)
        turned[head * QLEN : (head + 1) * QLEN, :] = query.astype(jnp.bfloat16)
    together = 2 if heads % 2 == 0 else 1
    height = together * QLEN
    row = lax.broadcasted_iota(jnp.int32, (height, QLEN), 0) % QLEN
    allowed = lax.broadcasted_iota(jnp.int32, (height, QLEN), 1) <= row
    for block in range(heads // together):
        scores = lax.dot_general(
            turned[block * height : (block + 1) * height, :],
            keys[...],
            (((1,), (1,)), ((), ())),
            preferred_element_type=jnp.float32,
        )
        own = jnp.where(allowed, scores[:, cached:], -1e30)
        scores = scores[:, :cached]
        row_max = jnp.maximum(
            jnp.max(scores, axis=1, keepdims=True), jnp.max(own, axis=1, keepdims=True)
        )
        weights = jnp.exp(scores - row_max)
        own = jnp.where(allowed, jnp.exp(own - row_max), 0.0)
        total = jnp.sum(weights, axis=1, keepdims=True) + jnp.sum(own, axis=1, keepdims=True)
        blended = jnp.dot(
            weights.astype(jnp.bfloat16), values[:cached, :], preferred_element_type=jnp.float32
        ) + jnp.dot(own.astype(jnp.bfloat16), values[cached:, :], preferred_element_type=jnp.float32)
        blended = (blended / total).astype(jnp.bfloat16)
        for i in range(together):
            head = block * together + i
            out[:, head * HD : (head + 1) * HD] = blended[i * QLEN : (i + 1) * QLEN, :]


def attend(ids, offsets, sums, scale, request_kv, stored, tables):
    requests, slots = ids.shape
    rows, cols = sums.shape
    total_keys = slots * PLEN + QLEN
    heads = cols // HD

    def per_request(width):
        return pl.BlockSpec((QLEN, width), lambda r, *_: (r, 0))

    def whole(array):
        return pl.BlockSpec(array.shape, lambda r, *_: (0, 0))

    products = rows * heads * total_keys
    return pl.pallas_call(
        attention_kernel,
        grid_spec=pltpu.PrefetchScalarGridSpec(
            num_scalar_prefetch=2,
            grid=(requests,),
            in_specs=[
                per_request(cols),
                per_request(1),
                per_request(2 * HD),
                whole(stored),
                whole(tables[0]),
                whole(tables[1]),
            ],
            out_specs=per_request(cols),
            scratch_shapes=[
                pltpu.VMEM((heads * QLEN, HD), jnp.bfloat16),
                pltpu.VMEM((total_keys, HD), jnp.bfloat16),
                pltpu.VMEM((total_keys, HD), jnp.bfloat16),
            ],
        ),
        out_shape=jax.ShapeDtypeStruct((rows, cols), jnp.bfloat16),
        compiler_params=pltpu.CompilerParams(vmem_limit_bytes=32 * 1024 * 1024),
        cost_estimate=pl.CostEstimate(
            flops=4 * products * HD, bytes_accessed=rows * cols * 6, transcendentals=products
        ),
        name="attention",
    )(ids, offsets, sums, scale, request_kv, stored, *tables)


def line_perms(n):
    depth = n // SIDE
    across = [(h, h ^ 1) for h in range(n)]
    return depth, across


def hop(value, n, senders, direction):
    perm = [
        (z * SIDE + y, (z + direction) * SIDE + y)
        for z in senders
        if 0 <= z + direction < n // SIDE
        for y in range(SIDE)
    ]
    return lax.ppermute(value, "head", perm)


def pick(index, choices):
    result = choices[0]
    left = [c for c in choices if c is not result]
    while left:
        array = left[0]
        mask = False
        for i, choice in enumerate(choices):
            if choice is array:
                mask = mask | (index == i)
        result = jnp.where(mask, array, result)
        left = [c for c in left if c is not array]
    return result


def table_at(index, values):
    result = jnp.int32(values[-1])
    for i in range(len(values) - 1):
        result = jnp.where(index == i, jnp.int32(values[i]), result)
    return result


def orders(depth):
    return [sorted(range(depth), key=lambda d, z=z: (-abs(d - z), d)) for z in range(depth)]


def tie(*trees):
    return lax.optimization_barrier(trees)


def fold(rows, height):
    if rows.shape[0] == height:
        return rows
    return jnp.concatenate(jnp.split(rows, rows.shape[0] // height, axis=0), axis=1)


def unfold(block, cols):
    if block.shape[1] == cols:
        return block
    return jnp.concatenate(jnp.split(block, block.shape[1] // cols, axis=1), axis=0)


def widen(array, cols):
    if array.shape[1] == cols:
        return array
    return jnp.pad(array, ((0, 0), (0, cols - array.shape[1])))


def join(arrays):
    return arrays[0] if len(arrays) == 1 else jnp.concatenate(arrays, axis=1)


def at_offset(z, depth, slots, offset):
    order = orders(depth)
    chosen = [
        slots[order[zz].index(zz + offset)] if 0 <= zz + offset < depth else None
        for zz in range(depth)
    ]
    known = [c for c in chosen if c is not None]
    return pick(z, [known[0] if c is None else c for c in chosen])


def at_distance(z, depth, slots, k):
    order = orders(depth)
    chosen = []
    for zz in range(depth):
        dest = zz + k if zz + k < depth else zz - k
        chosen.append(slots[order[zz].index(dest)] if 0 <= dest < depth else None)
    known = [c for c in chosen if c is not None]
    return pick(z, [known[0] if c is None else c for c in chosen])


def line_values(z, n, slots, k, came):
    depth = n // SIDE
    if 2 * k > depth - 1:
        value = at_distance(z, depth, slots, k)
        if came:
            value = value + jnp.where(z < depth - k, *came).astype(jnp.float32)
        value = value.astype(jnp.bfloat16)
        return value, value
    values = []
    for i in range(2):
        value = at_offset(z, depth, slots, -k if i else k)
        if came:
            value = value + came[i].astype(jnp.float32)
        values.append(value.astype(jnp.bfloat16))
    return tuple(values)


def project(part, squares_q, normed, passages, query_weight, kv_weight, n):
    depth, across = line_perms(n)
    features = part.shape[1]
    height = part.shape[0]
    cols = 2 * HD
    me = lax.axis_index("head")
    z, y = me // SIDE, me % SIDE
    other = 1 - y
    order = orders(depth)
    dest = [table_at(z, [order[zz][slot] for zz in range(depth)]) for slot in range(depth)]
    width = max(features, passages.shape[0] // height * SIDE * cols)
    arrivals = []
    for zz in range(depth):
        near = []
        for s in range(1, depth):
            if zz - s >= 0:
                near.append((s, True))
            if zz + s < depth:
                near.append((s, False))
        arrivals.append(near)

    def product(total, news):
        for came, owner in news:
            rows = lax.dynamic_slice_in_dim(query_weight, owner * features, features, 0)
            term = jnp.dot(came, rows, preferred_element_type=jnp.float32)
            total = term if total is None else total + term
        return total

    def kv_product(rows, start, count):
        weight = lax.dynamic_slice_in_dim(kv_weight, start, count, 1)
        return jnp.dot(rows, weight, preferred_element_type=jnp.float32)

    ups, downs, crossing = [part], [part], (part, z)
    total, news = None, [(part, me)]
    squares, partner = squares_q, 1
    p_slots, p_came = [], ()
    q_slots, q_came, q_give = [], (), None
    questions = part
    for t in range(1, depth + 2):
        to_y = []
        to_z = ([], [])
        if t <= depth:
            to_y.append(crossing[0])
        if t == 1:
            for side in to_z:
                side.append(widen(part, width))
        elif t <= depth:
            values = line_values(z, n, p_slots, depth - t + 1, p_came)
            gathered = (ups[-1], downs[-1])
            for i, place in enumerate((z, depth - 1 - z)):
                mine = widen(fold(values[i], height), width)
                to_z[i].append(jnp.where(place < t - 1, mine, widen(gathered[i], width)))
        else:
            p_total = p_slots[depth - 1]
            for array in p_came:
                p_total = p_total + array.astype(jnp.float32)
            first, second = jnp.split(p_total, 2, axis=1)
            p_keep = jnp.where(y == 0, first, second)
            to_y.append(fold(jnp.where(y == 0, second, first).astype(jnp.bfloat16), height))
        if t >= 2:
            to_y.append(q_give)
        if t >= 3:
            for side, value in zip(to_z, line_values(z, n, q_slots, depth - t + 2, q_came)):
                side.append(value)
        sends, squares, news_arrays, total, passages, questions, p_slots, q_slots = tie(
            [join(to_y), join(to_z[0]), join(to_z[1])],
            squares,
            [came for came, _ in news],
            [] if total is None else [total],
            passages,
            questions,
            p_slots,
            q_slots,
        )
        last = t > depth
        received = [
            lax.ppermute(sends[0], "head", across),
            hop(sends[1], n, range(depth), 1),
            hop(sends[2], n, range(depth), -1),
        ]
        summing = t >= 2 and partner < n
        if summing:
            received.append(
                lax.ppermute(squares, "head", [(h, h ^ partner) for h in range(n)])
            )
        if t == 1:
            passages, squares_p = normed(passages)
            squares = jnp.concatenate([squares_p, squares])
        total = product(total[0] if total else None, [(c, o) for c, (_, o) in zip(news_arrays, news)])
        new_p = [kv_product(passages, dest[t - 1] * SIDE * cols, SIDE * cols)] if t <= depth else []
        q_mine = []
        if t >= 2:
            q_mine = [kv_product(questions, (dest[t - 2] * SIDE + y) * cols, cols)]
        new_give = []
        if t <= depth:
            new_give = [
                kv_product(questions, (dest[t - 1] * SIDE + other) * cols, cols).astype(jnp.bfloat16)
            ]
        received, squares, total, new_p, q_mine, new_give = tie(
            received, squares, total, new_p, q_mine, new_give
        )
        if summing:
            squares = squares + received.pop()
            partner *= 2
        p_slots = p_slots + new_p
        q_give = new_give[0] if new_give else None
        taken = 0
        news = []
        if t <= depth:
            news.append((received[0][:, :features], crossing[1] * SIDE + other))
            taken = features
        else:
            taken = passages.shape[0] // height * cols
            p_came_y = unfold(received[0][:, :taken], cols)
        if t >= 2:
            q_slots = q_slots + [q_mine[0] + received[0][:, taken:].astype(jnp.float32)]
        if t < depth:
            ups.append(received[1][:, :features])
            downs.append(received[2][:, :features])
            slot = [arrivals[zz][t - 1] for zz in range(depth)]
            came = pick(z, [(ups if u else downs)[d] for d, u in slot])
            source = table_at(z, [zz - d if u else zz + d for zz, (d, u) in enumerate(slot)])
            crossing = (came, source)
            news.append((came, source * SIDE + y))
        if 2 <= t <= depth:
            used = passages.shape[0] // height * SIDE * cols
            p_came = tuple(unfold(r[:, :used], SIDE * cols) for r in received[1:])
        if t >= 3:
            q_came = tuple(r[:, (0 if last else width) :] for r in received[1:])
    q_total = q_slots[depth - 1]
    for array in q_came:
        q_total = q_total + array.astype(jnp.float32)
    return product(total, news), p_keep + p_came_y.astype(jnp.float32), q_total, squares


def scatter_sum(block_of, source, n):
    depth, across = line_perms(n)
    me = lax.axis_index("head")
    z, y = me // SIDE, me % SIDE
    order = orders(depth)
    dest = [
        table_at(z, [order[zz][slot] for zz in range(depth)]) * SIDE for slot in range(depth)
    ]
    slots, came = [], []
    give = block_of(source, dest[0] + 1 - y).astype(jnp.bfloat16)
    for turn in range(depth):
        sends = [give]
        if turn:
            sends += line_values(z, n, slots, depth - turn, came)
        sends, source, slots = tie(sends, source, slots)
        received = [lax.ppermute(sends[0], "head", across)]
        if turn:
            received.append(hop(sends[1], n, range(turn), 1))
            received.append(hop(sends[2], n, range(depth - turn, depth), -1))
        mine = block_of(source, dest[turn] + y)
        gives = []
        if turn + 1 < depth:
            gives = [block_of(source, dest[turn + 1] + 1 - y).astype(jnp.bfloat16)]
        received, mine, gives = tie(received, mine, gives)
        give = gives[0] if gives else None
        came = received[1:]
        slots = slots + [mine + received[0].astype(jnp.float32)]
    total = slots[depth - 1]
    for array in came:
        total = total + array.astype(jnp.float32)
    return total


def spread_heads(matrix, group_size):
    if group_size == 1:
        return matrix
    leading = matrix.shape[0]
    per_head = matrix.reshape(leading, KV_HEADS, 2 * HD)
    return jnp.repeat(per_head, group_size, axis=1).reshape(leading, KV_HEADS * group_size * 2 * HD)


def local(
    passage_states,
    question_states,
    norm_gain,
    query_weight,
    kv_weight,
    out_weight,
    passage_ids,
    slot_offsets,
):
    n = lax.axis_size("head")
    pas_rows = passage_states.shape[0]
    question_rows = question_states.shape[0]
    features = norm_gain.shape[0]
    group_size = n // KV_HEADS
    block_cols = kv_weight.shape[1] // n
    query_cols = query_weight.shape[1]

    def normed(states):
        rows = states.astype(jnp.float32)
        return (rows * norm_gain[None, :]).astype(jnp.bfloat16), jnp.sum(rows * rows, axis=1)

    gained_q, squares_q = normed(question_states)
    spread = spread_heads(kv_weight, group_size)
    query_sums, passage_sums, request_sums, squares = project(
        gained_q, squares_q, normed, passage_states, query_weight, spread, n
    )
    row_scale = lax.rsqrt(squares / D + 1e-05)[:, None]
    passage_kv = (row_scale[:pas_rows] * passage_sums).astype(jnp.bfloat16)
    request_kv = (row_scale[pas_rows:] * request_sums).astype(jnp.bfloat16)
    own_start = lax.axis_index("head") % group_size * block_cols
    passage_out = lax.dynamic_slice_in_dim(passage_kv, own_start, block_cols, 1)
    items = lax.axis_size("item")
    stored = [passage_kv]
    for _ in range(items - 1):
        ring = [(i, (i - 1) % items) for i in range(items)]
        stored.append(lax.ppermute(stored[-1], "item", ring))
    stored = jnp.concatenate(stored, axis=0)
    held = stored.shape[0] // PLEN
    place = (passage_ids - lax.axis_index("item") * (pas_rows // PLEN)) % held
    positions = jnp.arange(passage_ids.shape[1] * PLEN + QLEN, dtype=jnp.int32)
    attention = attend(
        place,
        slot_offsets,
        query_sums,
        row_scale[pas_rows:],
        request_kv,
        stored,
        rope_tables(positions),
    )

    def out_block(rows, device):
        columns = lax.dynamic_slice_in_dim(out_weight, device * features, features, 1)
        return jnp.dot(rows, columns, preferred_element_type=jnp.float32)

    summed = scatter_sum(out_block, attention, n)
    question_out = (question_states.astype(jnp.float32) + summed).astype(jnp.bfloat16)
    return (passage_out, question_out)


def solution(mesh):
    return jax.shard_map(
        local,
        mesh=mesh,
        in_specs=(
            P(("grp", "item"), "head"),
            P(("grp", "item"), "head"),
            P("head"),
            P(None, "head"),
            P("head", None),
            P("head", None),
            P(("grp", "item"), None),
            P(("grp", "item"), None),
        ),
        out_specs=(P(("grp", "item"), "head"), P(("grp", "item"), "head")),
        check_vma=False,
    )
```

```python
import math

import jax
import jax.numpy as jnp
from jax import lax
from jax.experimental import pallas as pl
from jax.experimental.pallas import tpu as pltpu
from jax.sharding import PartitionSpec as P

D = 8192
KV_HEADS = 8
HD = 128
PLEN = 256
QLEN = 128
HALVES = 2
SIDE = 2


def rope_tables(positions):
    half_dim = HD // 2
    inverse = jnp.exp(
        jnp.arange(half_dim, dtype=jnp.float32) * (-2.0 * math.log(500000.0) / HD)
    )
    angles = positions.astype(jnp.float32)[:, None] * inverse[None, :]
    cosine, sine_part = jnp.cos(angles), jnp.sin(angles)
    return (
        jnp.concatenate([cosine, cosine], axis=1),
        jnp.concatenate([-sine_part, sine_part], axis=1),
    )


def attention_kernel(
    ids, offsets, sums, scale, request_kv, stored, cosines, sines, out, turned, keys, values
):
    request = pl.program_id(0)
    slots = ids.shape[1]
    cached = slots * PLEN
    total_keys = cached + QLEN
    heads = sums.shape[1] // HD

    def rot(vectors, cosine, sine):
        return vectors * cosine + pltpu.roll(vectors, HD // 2, 1) * sine

    q_cos = cosines[pl.ds(cached, QLEN), :]
    q_sin = sines[pl.ds(cached, QLEN), :]
    for slot in range(slots):
        start = pl.multiple_of(ids[request, slot] * PLEN, PLEN)
        offset = offsets[request, slot]
        rows = slice(slot * PLEN, (slot + 1) * PLEN)
        key = stored[pl.ds(start, PLEN), :HD].astype(jnp.float32)
        key = rot(key, cosines[pl.ds(offset, PLEN), :], sines[pl.ds(offset, PLEN), :])
        keys[rows, :] = key.astype(jnp.bfloat16)
        values[rows, :] = stored[pl.ds(start, PLEN), HD:]
    key = rot(request_kv[:, :HD].astype(jnp.float32), q_cos, q_sin)
    keys[cached:, :] = key.astype(jnp.bfloat16)
    values[cached:, :] = request_kv[:, HD:]
    row_scale = scale[...]
    for head in range(heads):
        query = row_scale * sums[:, head * HD : (head + 1) * HD]
        query = rot(query, q_cos, q_sin) * HD ** (-0.5)
        turned[head * QLEN : (head + 1) * QLEN, :] = query.astype(jnp.bfloat16)
    together = 2 if heads % 2 == 0 else 1
    height = together * QLEN
    row = lax.broadcasted_iota(jnp.int32, (height, QLEN), 0) % QLEN
    allowed = lax.broadcasted_iota(jnp.int32, (height, QLEN), 1) <= row
    for block in range(heads // together):
        scores = lax.dot_general(
            turned[block * height : (block + 1) * height, :],
            keys[...],
            (((1,), (1,)), ((), ())),
            preferred_element_type=jnp.float32,
        )
        own = jnp.where(allowed, scores[:, cached:], -1e30)
        scores = scores[:, :cached]
        row_max = jnp.maximum(
            jnp.max(scores, axis=1, keepdims=True), jnp.max(own, axis=1, keepdims=True)
        )
        weights = jnp.exp(scores - row_max)
        own = jnp.where(allowed, jnp.exp(own - row_max), 0.0)
        total = jnp.sum(weights, axis=1, keepdims=True) + jnp.sum(own, axis=1, keepdims=True)
        blended = jnp.dot(
            weights.astype(jnp.bfloat16), values[:cached, :], preferred_element_type=jnp.float32
        ) + jnp.dot(own.astype(jnp.bfloat16), values[cached:, :], preferred_element_type=jnp.float32)
        blended = (blended / total).astype(jnp.bfloat16)
        for i in range(together):
            head = block * together + i
            out[:, head * HD : (head + 1) * HD] = blended[i * QLEN : (i + 1) * QLEN, :]


def attend(ids, offsets, sums, scale, request_kv, stored, tables, first):
    requests, slots = ids.shape
    rows, cols = requests * QLEN, sums.shape[1]
    total_keys = slots * PLEN + QLEN
    heads = cols // HD

    def per_request(width):
        return pl.BlockSpec((QLEN, width), lambda r, *_: (first + r, 0))

    def whole(array):
        return pl.BlockSpec(array.shape, lambda r, *_: (0, 0))

    products = rows * heads * total_keys
    return pl.pallas_call(
        attention_kernel,
        grid_spec=pltpu.PrefetchScalarGridSpec(
            num_scalar_prefetch=2,
            grid=(requests,),
            in_specs=[
                per_request(cols),
                per_request(1),
                per_request(2 * HD),
                whole(stored),
                whole(tables[0]),
                whole(tables[1]),
            ],
            out_specs=pl.BlockSpec((QLEN, cols), lambda r, *_: (r, 0)),
            scratch_shapes=[
                pltpu.VMEM((heads * QLEN, HD), jnp.bfloat16),
                pltpu.VMEM((total_keys, HD), jnp.bfloat16),
                pltpu.VMEM((total_keys, HD), jnp.bfloat16),
            ],
        ),
        out_shape=jax.ShapeDtypeStruct((rows, cols), jnp.bfloat16),
        compiler_params=pltpu.CompilerParams(vmem_limit_bytes=32 * 1024 * 1024),
        cost_estimate=pl.CostEstimate(
            flops=4 * products * HD, bytes_accessed=rows * cols * 6, transcendentals=products
        ),
        name="attention",
    )(ids, offsets, sums, scale, request_kv, stored, *tables)


def line_perms(n):
    depth = n // SIDE
    across = [(h, h ^ 1) for h in range(n)]
    return depth, across


def hop(value, n, senders, direction):
    perm = [
        (z * SIDE + y, (z + direction) * SIDE + y)
        for z in senders
        if 0 <= z + direction < n // SIDE
        for y in range(SIDE)
    ]
    return lax.ppermute(value, "head", perm)


def pick(index, choices):
    result = choices[0]
    left = [c for c in choices if c is not result]
    while left:
        array = left[0]
        mask = False
        for i, choice in enumerate(choices):
            if choice is array:
                mask = mask | (index == i)
        result = jnp.where(mask, array, result)
        left = [c for c in left if c is not array]
    return result


def table_at(index, values):
    result = jnp.int32(values[-1])
    for i in range(len(values) - 1):
        result = jnp.where(index == i, jnp.int32(values[i]), result)
    return result


def orders(depth):
    return [sorted(range(depth), key=lambda d, z=z: (-abs(d - z), d)) for z in range(depth)]


def tie(*trees):
    return lax.optimization_barrier(trees)


def fold(rows, height):
    if rows.shape[0] == height:
        return rows
    return jnp.concatenate(jnp.split(rows, rows.shape[0] // height, axis=0), axis=1)


def unfold(block, cols):
    if block.shape[1] == cols:
        return block
    return jnp.concatenate(jnp.split(block, block.shape[1] // cols, axis=1), axis=0)


def widen(array, cols):
    if array.shape[1] == cols:
        return array
    return jnp.pad(array, ((0, 0), (0, cols - array.shape[1])))


def join(arrays):
    return arrays[0] if len(arrays) == 1 else jnp.concatenate(arrays, axis=1)


def at_offset(z, depth, slots, offset):
    order = orders(depth)
    chosen = [
        slots[order[zz].index(zz + offset)] if 0 <= zz + offset < depth else None
        for zz in range(depth)
    ]
    known = [c for c in chosen if c is not None]
    return pick(z, [known[0] if c is None else c for c in chosen])


def at_distance(z, depth, slots, k):
    order = orders(depth)
    chosen = []
    for zz in range(depth):
        dest = zz + k if zz + k < depth else zz - k
        chosen.append(slots[order[zz].index(dest)] if 0 <= dest < depth else None)
    known = [c for c in chosen if c is not None]
    return pick(z, [known[0] if c is None else c for c in chosen])


def line_values(z, n, slots, k, came):
    depth = n // SIDE
    if 2 * k > depth - 1:
        value = at_distance(z, depth, slots, k)
        if came:
            value = value + jnp.where(z < depth - k, *came).astype(jnp.float32)
        value = value.astype(jnp.bfloat16)
        return value, value
    values = []
    for i in range(2):
        value = at_offset(z, depth, slots, -k if i else k)
        if came:
            value = value + came[i].astype(jnp.float32)
        values.append(value.astype(jnp.bfloat16))
    return tuple(values)


def project(part, squares_q, normed, passages, query_weight, kv_weight, n):
    depth, across = line_perms(n)
    features = part.shape[1]
    height = part.shape[0]
    cols = 2 * HD
    me = lax.axis_index("head")
    z, y = me // SIDE, me % SIDE
    other = 1 - y
    order = orders(depth)
    dest = [table_at(z, [order[zz][slot] for zz in range(depth)]) for slot in range(depth)]
    width = max(features, passages.shape[0] // height * SIDE * cols)
    arrivals = []
    for zz in range(depth):
        near = []
        for s in range(1, depth):
            if zz - s >= 0:
                near.append((s, True))
            if zz + s < depth:
                near.append((s, False))
        arrivals.append(near)

    def product(total, news):
        for came, owner in news:
            rows = lax.dynamic_slice_in_dim(query_weight, owner * features, features, 0)
            term = jnp.dot(came, rows, preferred_element_type=jnp.float32)
            total = term if total is None else total + term
        return total

    def kv_product(rows, start, count):
        weight = lax.dynamic_slice_in_dim(kv_weight, start, count, 1)
        return jnp.dot(rows, weight, preferred_element_type=jnp.float32)

    ups, downs, crossing = [part], [part], (part, z)
    total, news = None, [(part, me)]
    squares, partner = squares_q, 1
    p_slots, p_came = [], ()
    q_slots, q_came, q_give = [], (), None
    questions = part
    for t in range(1, depth + 2):
        to_y = []
        to_z = ([], [])
        if t <= depth:
            to_y.append(crossing[0])
        if t == 1:
            for side in to_z:
                side.append(widen(part, width))
        elif t <= depth:
            values = line_values(z, n, p_slots, depth - t + 1, p_came)
            gathered = (ups[-1], downs[-1])
            for i, place in enumerate((z, depth - 1 - z)):
                mine = widen(fold(values[i], height), width)
                to_z[i].append(jnp.where(place < t - 1, mine, widen(gathered[i], width)))
        else:
            p_total = p_slots[depth - 1]
            for array in p_came:
                p_total = p_total + array.astype(jnp.float32)
            first, second = jnp.split(p_total, 2, axis=1)
            p_keep = jnp.where(y == 0, first, second)
            to_y.append(fold(jnp.where(y == 0, second, first).astype(jnp.bfloat16), height))
        if t >= 2:
            to_y.append(q_give)
        if t >= 3:
            for side, value in zip(to_z, line_values(z, n, q_slots, depth - t + 2, q_came)):
                side.append(value)
        sends, squares, news_arrays, total, passages, questions, p_slots, q_slots = tie(
            [join(to_y), join(to_z[0]), join(to_z[1])],
            squares,
            [came for came, _ in news],
            [] if total is None else [total],
            passages,
            questions,
            p_slots,
            q_slots,
        )
        last = t > depth
        received = [
            lax.ppermute(sends[0], "head", across),
            hop(sends[1], n, range(depth), 1),
            hop(sends[2], n, range(depth), -1),
        ]
        summing = t >= 2 and partner < n
        if summing:
            received.append(
                lax.ppermute(squares, "head", [(h, h ^ partner) for h in range(n)])
            )
        if t == 1:
            passages, squares_p = normed(passages)
            squares = jnp.concatenate([squares_p, squares])
        total = product(total[0] if total else None, [(c, o) for c, (_, o) in zip(news_arrays, news)])
        new_p = [kv_product(passages, dest[t - 1] * SIDE * cols, SIDE * cols)] if t <= depth else []
        q_mine = []
        if t >= 2:
            q_mine = [kv_product(questions, (dest[t - 2] * SIDE + y) * cols, cols)]
        new_give = []
        if t <= depth:
            new_give = [
                kv_product(questions, (dest[t - 1] * SIDE + other) * cols, cols).astype(jnp.bfloat16)
            ]
        received, squares, total, new_p, q_mine, new_give = tie(
            received, squares, total, new_p, q_mine, new_give
        )
        if summing:
            squares = squares + received.pop()
            partner *= 2
        p_slots = p_slots + new_p
        q_give = new_give[0] if new_give else None
        taken = 0
        news = []
        if t <= depth:
            news.append((received[0][:, :features], crossing[1] * SIDE + other))
            taken = features
        else:
            taken = passages.shape[0] // height * cols
            p_came_y = unfold(received[0][:, :taken], cols)
        if t >= 2:
            q_slots = q_slots + [q_mine[0] + received[0][:, taken:].astype(jnp.float32)]
        if t < depth:
            ups.append(received[1][:, :features])
            downs.append(received[2][:, :features])
            slot = [arrivals[zz][t - 1] for zz in range(depth)]
            came = pick(z, [(ups if u else downs)[d] for d, u in slot])
            source = table_at(z, [zz - d if u else zz + d for zz, (d, u) in enumerate(slot)])
            crossing = (came, source)
            news.append((came, source * SIDE + y))
        if 2 <= t <= depth:
            used = passages.shape[0] // height * SIDE * cols
            p_came = tuple(unfold(r[:, :used], SIDE * cols) for r in received[1:])
        if t >= 3:
            q_came = tuple(r[:, (0 if last else width) :] for r in received[1:])
    q_total = q_slots[depth - 1]
    for array in q_came:
        q_total = q_total + array.astype(jnp.float32)
    return product(total, news), p_keep + p_came_y.astype(jnp.float32), q_total, squares


def scatter_sum(block_of, source, n):
    depth, across = line_perms(n)
    me = lax.axis_index("head")
    z, y = me // SIDE, me % SIDE
    order = orders(depth)
    dest = [
        table_at(z, [order[zz][slot] for zz in range(depth)]) * SIDE for slot in range(depth)
    ]
    slots, came = [], []
    give = block_of(source, dest[0] + 1 - y)
    for turn in range(depth):
        sends = [give]
        if turn:
            sends += line_values(z, n, slots, depth - turn, came)
        sends, source, slots = tie(sends, source, slots)
        received = [lax.ppermute(sends[0], "head", across)]
        if turn:
            received.append(hop(sends[1], n, range(turn), 1))
            received.append(hop(sends[2], n, range(depth - turn, depth), -1))
        mine = block_of(source, dest[turn] + y)
        gives = []
        if turn + 1 < depth:
            gives = [block_of(source, dest[turn + 1] + 1 - y)]
        yield
        received, mine, gives = tie(received, mine, gives)
        give = gives[0] if gives else None
        came = received[1:]
        slots = slots + [mine.astype(jnp.float32) + received[0].astype(jnp.float32)]
    total = slots[depth - 1]
    for array in came:
        total = total + array.astype(jnp.float32)
    return total


def interleave(generators):
    results = [None] * len(generators)
    live = list(range(len(generators)))
    while live:
        for i in list(live):
            try:
                next(generators[i])
            except StopIteration as stop:
                results[i] = stop.value
                live.remove(i)
    return results


def spread_heads(matrix, group_size):
    if group_size == 1:
        return matrix
    leading = matrix.shape[0]
    per_head = matrix.reshape(leading, KV_HEADS, 2 * HD)
    return jnp.repeat(per_head, group_size, axis=1).reshape(leading, KV_HEADS * group_size * 2 * HD)


def local(
    passage_states,
    question_states,
    norm_gain,
    query_weight,
    kv_weight,
    out_weight,
    passage_ids,
    slot_offsets,
):
    n = lax.axis_size("head")
    pas_rows = passage_states.shape[0]
    question_rows = question_states.shape[0]
    features = norm_gain.shape[0]
    group_size = n // KV_HEADS
    block_cols = kv_weight.shape[1] // n
    query_cols = query_weight.shape[1]

    def normed(states):
        rows = states.astype(jnp.float32)
        return (rows * norm_gain[None, :]).astype(jnp.bfloat16), jnp.sum(rows * rows, axis=1)

    gained_q, squares_q = normed(question_states)
    spread = spread_heads(kv_weight, group_size)
    query_sums, passage_sums, request_sums, squares = project(
        gained_q, squares_q, normed, passage_states, query_weight, spread, n
    )
    row_scale = lax.rsqrt(squares / D + 1e-05)[:, None]
    passage_kv = (row_scale[:pas_rows] * passage_sums).astype(jnp.bfloat16)
    request_kv = (row_scale[pas_rows:] * request_sums).astype(jnp.bfloat16)
    own_start = lax.axis_index("head") % group_size * block_cols
    passage_out = lax.dynamic_slice_in_dim(passage_kv, own_start, block_cols, 1)
    items = lax.axis_size("item")
    stored = [passage_kv]
    for _ in range(items - 1):
        ring = [(i, (i - 1) % items) for i in range(items)]
        stored.append(lax.ppermute(stored[-1], "item", ring))
    stored = jnp.concatenate(stored, axis=0)
    held = stored.shape[0] // PLEN
    place = (passage_ids - lax.axis_index("item") * (pas_rows // PLEN)) % held
    positions = jnp.arange(passage_ids.shape[1] * PLEN + QLEN, dtype=jnp.int32)
    tables = rope_tables(positions)

    def out_block(rows, device):
        columns = lax.dynamic_slice_in_dim(out_weight, device * features, features, 1)
        product = jnp.dot(rows, columns, preferred_element_type=jnp.float32)
        return product.astype(jnp.bfloat16)

    halves = HALVES if passage_ids.shape[0] % HALVES == 0 else 1
    requests = passage_ids.shape[0] // halves
    rows = requests * QLEN
    chains = []
    for half in range(halves):
        attention = attend(
            place[half * requests : (half + 1) * requests],
            slot_offsets[half * requests : (half + 1) * requests],
            query_sums,
            row_scale[pas_rows:],
            request_kv,
            stored,
            tables,
            half * requests,
        )
        chain = scatter_sum(out_block, attention, n)
        chains.append(chain)
    summed = jnp.concatenate(interleave(chains), axis=0)
    question_out = (question_states.astype(jnp.float32) + summed).astype(jnp.bfloat16)
    return (passage_out, question_out)


def solution(mesh):
    return jax.shard_map(
        local,
        mesh=mesh,
        in_specs=(
            P(("grp", "item"), "head"),
            P(("grp", "item"), "head"),
            P("head"),
            P(None, "head"),
            P("head", None),
            P("head", None),
            P(("grp", "item"), None),
            P(("grp", "item"), None),
        ),
        out_specs=(P(("grp", "item"), "head"), P(("grp", "item"), "head")),
        check_vma=False,
    )
```

```python
import math

import jax
import jax.numpy as jnp
from jax import lax
from jax.experimental import pallas as pl
from jax.experimental.pallas import tpu as pltpu
from jax.sharding import PartitionSpec as P

D = 8192
KV_HEADS = 8
HD = 128
PLEN = 256
QLEN = 128
SIDE = 2


def rope_tables(positions):
    lanes = jnp.arange(HD, dtype=jnp.int32)
    inverse = jnp.exp(
        (lanes % (HD // 2)).astype(jnp.float32) * (-2.0 * math.log(500000.0) / HD)
    )
    angles = positions.astype(jnp.float32)[:, None] * inverse[None, :]
    return jnp.cos(angles), jnp.where(lanes[None, :] < HD // 2, -jnp.sin(angles), jnp.sin(angles))


def attention_kernel(
    ids, offsets, sums, scale, request_kv, stored, cosines, sines, out, turned, keys, values
):
    request = pl.program_id(0)
    slots = ids.shape[1]
    cached = slots * PLEN
    total_keys = cached + QLEN
    heads = sums.shape[1] // HD

    def rot(vectors, cosine, sine):
        return vectors * cosine + pltpu.roll(vectors, HD // 2, 1) * sine

    q_cos = cosines[pl.ds(cached, QLEN), :]
    q_sin = sines[pl.ds(cached, QLEN), :]
    for slot in range(slots):
        start = pl.multiple_of(ids[request, slot] * PLEN, PLEN)
        offset = offsets[request, slot]
        rows = slice(slot * PLEN, (slot + 1) * PLEN)
        key = stored[pl.ds(start, PLEN), :HD].astype(jnp.float32)
        key = rot(key, cosines[pl.ds(offset, PLEN), :], sines[pl.ds(offset, PLEN), :])
        keys[rows, :] = key.astype(jnp.bfloat16)
        values[rows, :] = stored[pl.ds(start, PLEN), HD:]
    key = rot(request_kv[:, :HD].astype(jnp.float32), q_cos, q_sin)
    keys[cached:, :] = key.astype(jnp.bfloat16)
    values[cached:, :] = request_kv[:, HD:]
    row_scale = scale[...]
    for head in range(heads):
        query = row_scale * sums[:, head * HD : (head + 1) * HD]
        query = rot(query, q_cos, q_sin) * HD ** (-0.5)
        turned[head * QLEN : (head + 1) * QLEN, :] = query.astype(jnp.bfloat16)
    together = 2 if heads % 2 == 0 else 1
    height = together * QLEN
    row = lax.broadcasted_iota(jnp.int32, (height, QLEN), 0) % QLEN
    allowed = lax.broadcasted_iota(jnp.int32, (height, QLEN), 1) <= row
    for block in range(heads // together):
        scores = lax.dot_general(
            turned[block * height : (block + 1) * height, :],
            keys[...],
            (((1,), (1,)), ((), ())),
            preferred_element_type=jnp.float32,
        )
        own = jnp.where(allowed, scores[:, cached:], -1e30)
        scores = scores[:, :cached]
        row_max = jnp.maximum(
            jnp.max(scores, axis=1, keepdims=True), jnp.max(own, axis=1, keepdims=True)
        )
        weights = jnp.exp(scores - row_max)
        own = jnp.where(allowed, jnp.exp(own - row_max), 0.0)
        total = jnp.sum(weights, axis=1, keepdims=True) + jnp.sum(own, axis=1, keepdims=True)
        blended = jnp.dot(
            weights.astype(jnp.bfloat16), values[:cached, :], preferred_element_type=jnp.float32
        ) + jnp.dot(own.astype(jnp.bfloat16), values[cached:, :], preferred_element_type=jnp.float32)
        blended = (blended / total).astype(jnp.bfloat16)
        for i in range(together):
            head = block * together + i
            out[:, head * HD : (head + 1) * HD] = blended[i * QLEN : (i + 1) * QLEN, :]


def attend(ids, offsets, sums, scale, request_kv, stored, tables, first):
    requests, slots = ids.shape
    rows, cols = requests * QLEN, sums.shape[1]
    total_keys = slots * PLEN + QLEN
    heads = cols // HD

    def per_request(width, skipped=0):
        return pl.BlockSpec((QLEN, width), lambda r, *_: (skipped + first + r, 0))

    def whole(array):
        return pl.BlockSpec(array.shape, lambda r, *_: (0, 0))

    return pl.pallas_call(
        attention_kernel,
        grid_spec=pltpu.PrefetchScalarGridSpec(
            num_scalar_prefetch=2,
            grid=(requests,),
            in_specs=[
                per_request(cols),
                per_request(1, (scale.shape[0] - sums.shape[0]) // QLEN),
                per_request(2 * HD),
                whole(stored),
                whole(tables[0]),
                whole(tables[1]),
            ],
            out_specs=pl.BlockSpec((QLEN, cols), lambda r, *_: (r, 0)),
            scratch_shapes=[
                pltpu.VMEM((heads * QLEN, HD), jnp.bfloat16),
                pltpu.VMEM((total_keys, HD), jnp.bfloat16),
                pltpu.VMEM((total_keys, HD), jnp.bfloat16),
            ],
        ),
        out_shape=jax.ShapeDtypeStruct((rows, cols), jnp.bfloat16),
        compiler_params=pltpu.CompilerParams(vmem_limit_bytes=32 * 1024 * 1024),
        cost_estimate=pl.CostEstimate(flops=1, bytes_accessed=1, transcendentals=0),
        name="attention",
    )(ids, offsets, sums, scale, request_kv, stored, *tables)


def swap(value, n, link, distance=None):
    depth = n // SIDE
    perm = []
    for z in range(depth):
        way = 1 if z % 2 == link else -1
        if 0 <= z + way < depth and (distance is None or 0 <= z + way * distance < depth):
            perm += [(z * SIDE + y, (z + way) * SIDE + y) for y in range(SIDE)]
    return lax.ppermute(value, "head", perm)


def cross(value, n):
    return lax.ppermute(value, "head", [(h, h ^ 1) for h in range(n)])


def pick(index, choices):
    arrays = []
    for choice in choices:
        if choice is not None and not any(choice is a for a in arrays):
            arrays.append(choice)
    result = arrays[0]
    for array in arrays[1:]:
        mask = False
        for i, choice in enumerate(choices):
            if choice is array:
                mask = mask | (index == i)
        result = jnp.where(mask, array, result)
    return result


def table_at(index, values):
    result = jnp.int32(values[-1])
    for i in range(len(values) - 1):
        result = jnp.where(index == i, jnp.int32(values[i]), result)
    return result


def orders(depth):
    def key(z, d):
        return -abs(d - z), (d > z) == (z % 2 == 0)

    return [sorted(range(depth), key=lambda d, z=z: key(z, d)) for z in range(depth)]


def arrivals(depth):
    result = []
    for z in range(depth):
        near = []
        for s in range(1, depth):
            for link in range(2):
                way = 1 if z % 2 == link else -1
                if 0 <= z + way * s < depth:
                    near.append((s, link))
        result.append(near)
    return result


def tie(*trees):
    return lax.optimization_barrier(trees)


def fold(rows, height):
    if rows.shape[0] == height:
        return rows
    return jnp.concatenate(jnp.split(rows, rows.shape[0] // height, axis=0), axis=1)


def unfold(block, cols):
    if block.shape[1] == cols:
        return block
    return jnp.concatenate(jnp.split(block, block.shape[1] // cols, axis=1), axis=0)


def widen(array, cols):
    if array.shape[1] == cols:
        return array
    return jnp.pad(array, ((0, 0), (0, cols - array.shape[1])))


def join(arrays):
    return arrays[0] if len(arrays) == 1 else jnp.concatenate(arrays, axis=1)


def line_values(z, depth, slots, k, came):
    order = orders(depth)
    values = []
    for link in range(2):
        chosen = []
        for zz in range(depth):
            d = zz + k if zz % 2 == link else zz - k
            chosen.append(slots[order[zz].index(d)] if 0 <= d < depth else None)
        if all(c is None for c in chosen):
            continue
        value = pick(z, chosen)
        if len(came) > 1 - link:
            value = value + came[1 - link].astype(jnp.float32)
        values.append(value.astype(jnp.bfloat16))
    return values


def project(part, squares_q, normed, passages, tables, query_weight, kv_weight, n):
    depth = n // SIDE
    height, features = part.shape
    cols = 2 * HD
    me = lax.axis_index("head")
    z, y = me // SIDE, me % SIDE
    other = 1 - y
    order = orders(depth)
    near = arrivals(depth)
    dest = [table_at(z, [order[zz][slot] for zz in range(depth)]) for slot in range(depth)]
    blocks = passages.shape[0] // height
    width = max(features, blocks * SIDE * cols)
    behind = [jnp.where(z % 2 == link, z, depth - 1 - z) for link in range(2)]

    def product(total, news):
        for came, owner in news:
            rows = lax.dynamic_slice_in_dim(query_weight, owner * features, features, 0)
            term = jnp.dot(came, rows, preferred_element_type=jnp.float32)
            total = term if total is None else total + term
        return total

    def kv_product(rows, start, count):
        weight = lax.dynamic_slice_in_dim(kv_weight, start, count, 1)
        return jnp.dot(rows, weight, preferred_element_type=jnp.float32)

    went = [[part, part]]
    crossing = (part, z)
    total, news = None, [(part, me)]
    squares, partner = squares_q, 1
    p_slots, p_came = [], ()
    q_slots, q_came, q_give = [], (), None
    questions = part
    for t in range(1, depth + 2):
        to_y, to_z = [], [[], []]
        if t <= depth:
            to_y.append(crossing[0])
        if t == 1:
            to_z = [[widen(part, width)], [widen(part, width)]]
        elif t <= depth:
            values = line_values(z, depth, p_slots, depth - t + 1, p_came)
            for link in range(2):
                mine = widen(fold(values[min(link, len(values) - 1)], height), width)
                gathered = widen(went[-1][1 - link], width)
                to_z[link].append(jnp.where(behind[link] < t - 1, mine, gathered))
        else:
            p_total = p_slots[depth - 1]
            for array in p_came:
                p_total = p_total + array.astype(jnp.float32)
            left, right = jnp.split(p_total, 2, axis=1)
            p_keep = jnp.where(y == 0, left, right)
            to_y.append(fold(jnp.where(y == 0, right, left).astype(jnp.bfloat16), height))
        if t >= 2:
            to_y.append(q_give)
        if t >= 3:
            values = line_values(z, depth, q_slots, depth - t + 2, q_came)
            for link in range(2):
                to_z[link].append(values[min(link, len(values) - 1)])
        sends, late, news_arrays, total, passages, questions, p_slots, q_slots = tie(
            [join(to_y), join(to_z[0]), join(to_z[1])],
            [squares] if t >= 2 else [],
            [came for came, _ in news],
            [] if total is None else [total],
            passages,
            questions,
            p_slots,
            q_slots,
        )
        received = [cross(sends[0], n), swap(sends[1], n, 0), swap(sends[2], n, 1)]
        if late:
            squares = late[0]
        summing = t >= 2 and partner < n
        if summing:
            received.append(
                lax.ppermute(squares, "head", [(h, h ^ partner) for h in range(n)])
            )
        if t == 1:
            passages, squares_p = normed(passages)
            squares = jnp.concatenate([squares_p, squares])
        total = product(total[0] if total else None, [(c, o) for c, (_, o) in zip(news_arrays, news)])
        new_p = [kv_product(passages, dest[t - 1] * SIDE * cols, SIDE * cols)] if t <= depth else []
        q_mine = []
        if t >= 2:
            q_mine = [kv_product(questions, (dest[t - 2] * SIDE + y) * cols, cols)]
        new_give = []
        if t <= depth:
            new_give = [
                kv_product(questions, (dest[t - 1] * SIDE + other) * cols, cols).astype(jnp.bfloat16)
            ]
        received, squares, total, new_p, q_mine, new_give = tie(
            received, squares, total, new_p, q_mine, new_give
        )
        if t == 2:
            received, tables = tie(received, tables)
        if summing:
            squares = squares + received.pop()
            partner *= 2
        p_slots = p_slots + new_p
        q_give = new_give[0] if new_give else None
        news = []
        if t <= depth:
            taken = features
            news.append((received[0][:, :features], crossing[1] * SIDE + other))
        else:
            taken = blocks * cols
            p_came_y = unfold(received[0][:, :taken], cols)
        if t >= 2:
            q_slots = q_slots + [q_mine[0] + received[0][:, taken:].astype(jnp.float32)]
        if t < depth:
            went.append([array[:, :features] for array in received[1:]])
            slot = [near[zz][t - 1] for zz in range(depth)]
            came = pick(z, [went[s][link] for s, link in slot])
            source = table_at(
                z, [zz + s if zz % 2 == link else zz - s for zz, (s, link) in enumerate(slot)]
            )
            crossing = (came, source)
            news.append((came, source * SIDE + y))
        if 2 <= t <= depth:
            used = blocks * SIDE * cols
            p_came = [unfold(array[:, :used], SIDE * cols) for array in received[1:]]
        if t >= 3:
            q_came = [array[:, (width if t <= depth else 0) :] for array in received[1:]]
    q_total = q_slots[depth - 1]
    for array in q_came:
        q_total = q_total + array.astype(jnp.float32)
    passage_sums = p_keep + p_came_y.astype(jnp.float32)
    return product(total, news), passage_sums, q_total, squares, tables


def scatter_sum(block_of, source, n, held=None, later=None):
    depth = n // SIDE
    me = lax.axis_index("head")
    z, y = me // SIDE, me % SIDE
    order = orders(depth)
    dest = [
        table_at(z, [order[zz][slot] for zz in range(depth)]) * SIDE for slot in range(depth)
    ]
    slots, came = [], []
    give = block_of(source, dest[0] + 1 - y)
    source = source if later is None else later
    for turn in range(depth):
        sends = [give]
        if turn:
            sends += line_values(z, depth, slots, depth - turn, came)
        sends, source, slots, held = tie(sends, source, slots, held)
        received = [cross(sends[0], n)]
        for link, value in enumerate(sends[1:]):
            received.append(swap(value, n, link, depth - turn))
        mine = block_of(source, dest[turn] + y)
        gives = []
        if turn + 1 < depth:
            gives = [block_of(source, dest[turn + 1] + 1 - y)]
        held = yield held
        received, mine, gives, held = tie(received, mine, gives, held)
        give = gives[0] if gives else None
        came = received[1:]
        slots = slots + [mine.astype(jnp.float32) + received[0].astype(jnp.float32)]
    total = slots[depth - 1]
    for array in came:
        total = total + array.astype(jnp.float32)
    return total


def interleave(generators):
    results = [None] * len(generators)
    live = list(range(len(generators)))
    while live:
        for i in list(live):
            try:
                next(generators[i])
            except StopIteration as stop:
                results[i] = stop.value
                live.remove(i)
    return results


def spread_heads(matrix, group_size):
    if group_size == 1:
        return matrix
    leading = matrix.shape[0]
    per_head = matrix.reshape(leading, KV_HEADS, 2 * HD)
    return jnp.repeat(per_head, group_size, axis=1).reshape(leading, KV_HEADS * group_size * 2 * HD)


def local(
    passage_states,
    question_states,
    norm_gain,
    query_weight,
    kv_weight,
    out_weight,
    passage_ids,
    slot_offsets,
):
    n = lax.axis_size("head")
    pas_rows = passage_states.shape[0]
    question_rows = question_states.shape[0]
    features = norm_gain.shape[0]
    group_size = n // KV_HEADS
    block_cols = kv_weight.shape[1] // n
    query_cols = query_weight.shape[1]

    def normed(states):
        rows = states.astype(jnp.float32)
        return (rows * norm_gain[None, :]).astype(jnp.bfloat16), jnp.sum(rows * rows, axis=1)

    gained_q, squares_q = normed(question_states)
    spread = spread_heads(kv_weight, group_size)
    positions = jnp.arange(passage_ids.shape[1] * PLEN + QLEN, dtype=jnp.int32)
    tables = rope_tables(positions)
    query_sums, passage_sums, request_sums, squares, tables = project(
        gained_q, squares_q, normed, passage_states, tables, query_weight, spread, n
    )
    row_scale = lax.rsqrt(squares / D + 1e-05)[:, None]
    passage_kv = (row_scale[:pas_rows] * passage_sums).astype(jnp.bfloat16)
    request_kv = (row_scale[pas_rows:] * request_sums).astype(jnp.bfloat16)
    own_start = lax.axis_index("head") % group_size * block_cols
    passage_out = lax.dynamic_slice_in_dim(passage_kv, own_start, block_cols, 1)
    items = lax.axis_size("item")
    stored = [passage_kv]
    for _ in range(items - 1):
        ring = [(i, (i - 1) % items) for i in range(items)]
        stored.append(lax.ppermute(stored[-1], "item", ring))
    stored = jnp.concatenate(stored, axis=0)
    held = stored.shape[0] // PLEN
    place = (passage_ids - lax.axis_index("item") * (pas_rows // PLEN)) % held
    def out_block(rows, device):
        columns = lax.dynamic_slice_in_dim(out_weight, device * features, features, 1)
        product = jnp.dot(rows, columns, preferred_element_type=jnp.float32)
        return product.astype(jnp.bfloat16)

    requests = passage_ids.shape[0] // 2

    def attention_of(half, stored):
        rows = slice(half * requests, (half + 1) * requests)
        return attend(
            place[rows],
            slot_offsets[rows],
            query_sums,
            row_scale,
            request_kv,
            stored,
            tables,
            half * requests,
        )

    first = scatter_sum(out_block, attention_of(0, stored), n, stored)
    attention = attention_of(1, next(first))
    second = scatter_sum(out_block, attention, n, None, first.send(attention))
    summed = jnp.concatenate(interleave([second, first])[::-1], axis=0)
    question_out = (question_states.astype(jnp.float32) + summed).astype(jnp.bfloat16)
    return (passage_out, question_out)


def solution(mesh):
    return jax.shard_map(
        local,
        mesh=mesh,
        in_specs=(
            P(("grp", "item"), "head"),
            P(("grp", "item"), "head"),
            P("head"),
            P(None, "head"),
            P("head", None),
            P("head", None),
            P(("grp", "item"), None),
            P(("grp", "item"), None),
        ),
        out_specs=(P(("grp", "item"), "head"), P(("grp", "item"), "head")),
        check_vma=False,
    )
```

```python
import math

import jax
import jax.numpy as jnp
from jax import lax
from jax.experimental import pallas as pl
from jax.experimental.pallas import tpu as pltpu
from jax.sharding import PartitionSpec as P

D = 8192
KV_HEADS = 8
HD = 128
PLEN = 256
QLEN = 128
SIDE = 2


def rope_tables(positions):
    lanes = jnp.arange(HD, dtype=jnp.int32)
    inverse = jnp.exp(
        (lanes % (HD // 2)).astype(jnp.float32) * (-2.0 * math.log(500000.0) / HD)
    )
    angles = positions.astype(jnp.float32)[:, None] * inverse[None, :]
    return jnp.cos(angles), jnp.where(lanes[None, :] < HD // 2, -jnp.sin(angles), jnp.sin(angles))


def attention_kernel(
    ids, offsets, sums, scale, request_kv, stored, cosines, sines, out, turned, keys, values
):
    request = pl.program_id(0)
    slots = ids.shape[1]
    cached = slots * PLEN
    total_keys = cached + QLEN
    heads = sums.shape[1] // HD

    def rot(vectors, cosine, sine):
        return vectors * cosine + pltpu.roll(vectors, HD // 2, 1) * sine

    q_cos = cosines[pl.ds(cached, QLEN), :]
    q_sin = sines[pl.ds(cached, QLEN), :]
    for slot in range(slots):
        start = pl.multiple_of(ids[request, slot] * PLEN, PLEN)
        offset = offsets[request, slot]
        rows = slice(slot * PLEN, (slot + 1) * PLEN)
        key = stored[pl.ds(start, PLEN), :HD].astype(jnp.float32)
        key = rot(key, cosines[pl.ds(offset, PLEN), :], sines[pl.ds(offset, PLEN), :])
        keys[rows, :] = key.astype(jnp.bfloat16)
        values[rows, :] = stored[pl.ds(start, PLEN), HD:]
    key = rot(request_kv[:, :HD].astype(jnp.float32), q_cos, q_sin)
    keys[cached:, :] = key.astype(jnp.bfloat16)
    values[cached:, :] = request_kv[:, HD:]
    row_scale = scale[...]
    for head in range(heads):
        query = row_scale * sums[:, head * HD : (head + 1) * HD]
        query = rot(query, q_cos, q_sin) * HD ** (-0.5)
        turned[head * QLEN : (head + 1) * QLEN, :] = query.astype(jnp.bfloat16)
    together = 2 if heads % 2 == 0 else 1
    height = together * QLEN
    row = lax.broadcasted_iota(jnp.int32, (height, QLEN), 0) % QLEN
    allowed = lax.broadcasted_iota(jnp.int32, (height, QLEN), 1) <= row
    for block in range(heads // together):
        scores = lax.dot_general(
            turned[block * height : (block + 1) * height, :],
            keys[...],
            (((1,), (1,)), ((), ())),
            preferred_element_type=jnp.float32,
        )
        own = jnp.where(allowed, scores[:, cached:], -1e30)
        scores = scores[:, :cached]
        row_max = jnp.maximum(
            jnp.max(scores, axis=1, keepdims=True), jnp.max(own, axis=1, keepdims=True)
        )
        weights = jnp.exp(scores - row_max)
        own = jnp.where(allowed, jnp.exp(own - row_max), 0.0)
        total = jnp.sum(weights, axis=1, keepdims=True) + jnp.sum(own, axis=1, keepdims=True)
        blended = jnp.dot(
            weights.astype(jnp.bfloat16), values[:cached, :], preferred_element_type=jnp.float32
        ) + jnp.dot(own.astype(jnp.bfloat16), values[cached:, :], preferred_element_type=jnp.float32)
        blended = (blended / total).astype(jnp.bfloat16)
        for i in range(together):
            head = block * together + i
            out[:, head * HD : (head + 1) * HD] = blended[i * QLEN : (i + 1) * QLEN, :]


def attend(ids, offsets, sums, scale, request_kv, stored, tables, first):
    requests, slots = ids.shape
    rows, cols = requests * QLEN, sums.shape[1]
    total_keys = slots * PLEN + QLEN
    heads = cols // HD

    def per_request(width, skipped=0):
        return pl.BlockSpec((QLEN, width), lambda r, *_: (skipped + first + r, 0))

    def whole(array):
        return pl.BlockSpec(array.shape, lambda r, *_: (0, 0))

    return pl.pallas_call(
        attention_kernel,
        grid_spec=pltpu.PrefetchScalarGridSpec(
            num_scalar_prefetch=2,
            grid=(requests,),
            in_specs=[
                per_request(cols),
                per_request(1, (scale.shape[0] - sums.shape[0]) // QLEN),
                per_request(2 * HD),
                whole(stored),
                whole(tables[0]),
                whole(tables[1]),
            ],
            out_specs=pl.BlockSpec((QLEN, cols), lambda r, *_: (r, 0)),
            scratch_shapes=[
                pltpu.VMEM((heads * QLEN, HD), jnp.bfloat16),
                pltpu.VMEM((total_keys, HD), jnp.bfloat16),
                pltpu.VMEM((total_keys, HD), jnp.bfloat16),
            ],
        ),
        out_shape=jax.ShapeDtypeStruct((rows, cols), jnp.bfloat16),
        compiler_params=pltpu.CompilerParams(vmem_limit_bytes=32 * 1024 * 1024),
        cost_estimate=pl.CostEstimate(flops=1, bytes_accessed=1, transcendentals=0),
        name="attention",
    )(ids, offsets, sums, scale, request_kv, stored, *tables)


def swap(value, n, link, distance=None):
    depth = n // SIDE
    perm = []
    for z in range(depth):
        way = 1 if z % 2 == link else -1
        if 0 <= z + way < depth and (distance is None or 0 <= z + way * distance < depth):
            perm += [(z * SIDE + y, (z + way) * SIDE + y) for y in range(SIDE)]
    return lax.ppermute(value, "head", perm)


def cross(value, n):
    return lax.ppermute(value, "head", [(h, h ^ 1) for h in range(n)])


def pick(index, choices):
    arrays = []
    for choice in choices:
        if choice is not None and not any(choice is a for a in arrays):
            arrays.append(choice)
    result = arrays[0]
    for array in arrays[1:]:
        mask = False
        for i, choice in enumerate(choices):
            if choice is array:
                mask = mask | (index == i)
        result = jnp.where(mask, array, result)
    return result


def table_at(index, values):
    result = jnp.int32(values[-1])
    for i in range(len(values) - 1):
        result = jnp.where(index == i, jnp.int32(values[i]), result)
    return result


def orders(depth):
    def key(z, d):
        return -abs(d - z), (d > z) == (z % 2 == 0)

    return [sorted(range(depth), key=lambda d, z=z: key(z, d)) for z in range(depth)]


def arrivals(depth):
    result = []
    for z in range(depth):
        near = []
        for s in range(1, depth):
            for link in range(2):
                way = 1 if z % 2 == link else -1
                if 0 <= z + way * s < depth:
                    near.append((s, link))
        result.append(near)
    return result


def tie(*trees):
    return lax.optimization_barrier(trees)


def fold(rows, height):
    if rows.shape[0] == height:
        return rows
    return jnp.concatenate(jnp.split(rows, rows.shape[0] // height, axis=0), axis=1)


def unfold(block, cols):
    if block.shape[1] == cols:
        return block
    return jnp.concatenate(jnp.split(block, block.shape[1] // cols, axis=1), axis=0)


def widen(array, cols):
    if array.shape[1] == cols:
        return array
    return jnp.pad(array, ((0, 0), (0, cols - array.shape[1])))


def join(arrays):
    return arrays[0] if len(arrays) == 1 else jnp.concatenate(arrays, axis=1)


def line_values(z, depth, slots, k, came):
    order = orders(depth)
    values = []
    for link in range(2):
        chosen = []
        for zz in range(depth):
            d = zz + k if zz % 2 == link else zz - k
            chosen.append(slots[order[zz].index(d)] if 0 <= d < depth else None)
        if all(c is None for c in chosen):
            continue
        value = pick(z, chosen)
        if len(came) > 1 - link:
            value = value + came[1 - link].astype(jnp.float32)
        values.append(value.astype(jnp.bfloat16))
    return values


def project(part, squares_q, normed, passages, tables, query_weight, kv_weight, n):
    depth = n // SIDE
    height, features = part.shape
    cols = 2 * HD
    me = lax.axis_index("head")
    z, y = me // SIDE, me % SIDE
    other = 1 - y
    order = orders(depth)
    near = arrivals(depth)
    dest = [table_at(z, [order[zz][slot] for zz in range(depth)]) for slot in range(depth)]
    blocks = passages.shape[0] // height
    width = max(features, blocks * SIDE * cols)
    behind = [jnp.where(z % 2 == link, z, depth - 1 - z) for link in range(2)]

    def product(total, news):
        for came, owner in news:
            rows = lax.dynamic_slice_in_dim(query_weight, owner * features, features, 0)
            term = jnp.dot(came, rows, preferred_element_type=jnp.float32)
            total = term if total is None else total + term
        return total

    def kv_product(rows, start, count):
        weight = lax.dynamic_slice_in_dim(kv_weight, start, count, 1)
        return jnp.dot(rows, weight, preferred_element_type=jnp.float32)

    went = [[part, part]]
    crossing = (part, z)
    total, news = None, [(part, me)]
    squares, partner = squares_q, 1
    p_slots, p_came = [], ()
    q_slots, q_came, q_give = [], (), None
    questions = part
    for t in range(1, depth + 2):
        to_y, to_z = [], [[], []]
        if t <= depth:
            to_y.append(crossing[0])
        if t == 1:
            to_z = [[widen(part, width)], [widen(part, width)]]
        elif t <= depth:
            values = line_values(z, depth, p_slots, depth - t + 1, p_came)
            for link in range(2):
                payload = widen(went[-1][1 - link], width)
                if link < len(values):
                    mine = widen(fold(values[link], height), width)
                    payload = jnp.where(behind[link] < t - 1, mine, payload)
                to_z[link].append(payload)
        else:
            p_total = p_slots[depth - 1]
            for array in p_came:
                p_total = p_total + array.astype(jnp.float32)
            left, right = jnp.split(p_total, 2, axis=1)
            p_keep = jnp.where(y == 0, left, right)
            to_y.append(fold(jnp.where(y == 0, right, left).astype(jnp.bfloat16), height))
        alone = [q_give] if t >= 2 else []
        if t >= 3:
            values = line_values(z, depth, q_slots, depth - t + 2, q_came)
            for link, value in enumerate(values):
                to_z[link].append(value)
        sends, late, news_arrays, total, passages, questions, p_slots, q_slots = tie(
            [join(to_y), join(to_z[0]), join(to_z[1])] + alone,
            [squares] if t >= 2 else [],
            [came for came, _ in news],
            [] if total is None else [total],
            passages,
            questions,
            p_slots,
            q_slots,
        )
        received = [cross(sends[0], n), swap(sends[1], n, 0), swap(sends[2], n, 1)]
        if late:
            squares = late[0]
        summing = t >= 2 and partner < n
        q_came_y = [cross(array, n) for array in sends[3:]]
        if t == 1:
            passages, squares_p = normed(passages)
            squares = jnp.concatenate([squares_p, squares])
        total = product(total[0] if total else None, [(c, o) for c, (_, o) in zip(news_arrays, news)])
        new_p = [kv_product(passages, dest[t - 1] * SIDE * cols, SIDE * cols)] if t <= depth else []
        if summing and new_p:
            squares, new_p = tie(squares, new_p)
        if summing:
            received.append(lax.ppermute(squares, "head", [(h, h ^ partner) for h in range(n)]))
        q_mine = []
        if t >= 2:
            q_mine = [kv_product(questions, (dest[t - 2] * SIDE + y) * cols, cols)]
        new_give = []
        if t <= depth:
            new_give = [
                kv_product(questions, (dest[t - 1] * SIDE + other) * cols, cols).astype(jnp.bfloat16)
            ]
        received, q_came_y, squares, total, new_p, q_mine, new_give = tie(
            received, q_came_y, squares, total, new_p, q_mine, new_give
        )
        if t == 2:
            received, tables = tie(received, tables)
        if summing:
            squares = squares + received.pop()
            partner *= 2
        p_slots = p_slots + new_p
        q_give = new_give[0] if new_give else None
        news = []
        if t <= depth:
            news.append((received[0][:, :features], crossing[1] * SIDE + other))
        else:
            p_came_y = unfold(received[0], cols)
        if t >= 2:
            q_slots = q_slots + [q_mine[0] + q_came_y[0].astype(jnp.float32)]
        if t < depth:
            went.append([array[:, :features] for array in received[1:]])
            slot = [near[zz][t - 1] for zz in range(depth)]
            came = pick(z, [went[s][link] for s, link in slot])
            source = table_at(
                z, [zz + s if zz % 2 == link else zz - s for zz, (s, link) in enumerate(slot)]
            )
            crossing = (came, source)
            news.append((came, source * SIDE + y))
        if 2 <= t <= depth:
            used = blocks * SIDE * cols
            p_came = [unfold(array[:, :used], SIDE * cols) for array in received[1:]]
        if t >= 3:
            q_came = [array[:, (width if t <= depth else 0) :] for array in received[1:]]
            q_came = [array for array in q_came if array.shape[1]]
    q_total = q_slots[depth - 1]
    for array in q_came:
        q_total = q_total + array.astype(jnp.float32)
    passage_sums = p_keep + p_came_y.astype(jnp.float32)
    return product(total, news), passage_sums, q_total, squares, tables


def scatter_sum(block_of, source, n, held=None, later=None):
    depth = n // SIDE
    me = lax.axis_index("head")
    z, y = me // SIDE, me % SIDE
    order = orders(depth)
    dest = [
        table_at(z, [order[zz][slot] for zz in range(depth)]) * SIDE for slot in range(depth)
    ]
    slots, came = [], []
    give = block_of(source, dest[0] + 1 - y)
    source = source if later is None else later
    for turn in range(depth):
        sends = [give]
        if turn:
            sends += line_values(z, depth, slots, depth - turn, came)
        sends, source, slots, held = tie(sends, source, slots, held)
        received = [cross(sends[0], n)]
        for link, value in enumerate(sends[1:]):
            received.append(swap(value, n, link, depth - turn))
        mine = block_of(source, dest[turn] + y)
        gives = []
        if turn + 1 < depth:
            gives = [block_of(source, dest[turn + 1] + 1 - y)]
        held = yield held
        received, mine, gives, held = tie(received, mine, gives, held)
        give = gives[0] if gives else None
        came = received[1:]
        slots = slots + [mine.astype(jnp.float32) + received[0].astype(jnp.float32)]
    total = slots[depth - 1]
    for array in came:
        total = total + array.astype(jnp.float32)
    return total


def interleave(generators):
    results = [None] * len(generators)
    live = list(range(len(generators)))
    while live:
        for i in list(live):
            try:
                next(generators[i])
            except StopIteration as stop:
                results[i] = stop.value
                live.remove(i)
    return results


def spread_heads(matrix, group_size):
    if group_size == 1:
        return matrix
    leading = matrix.shape[0]
    per_head = matrix.reshape(leading, KV_HEADS, 2 * HD)
    return jnp.repeat(per_head, group_size, axis=1).reshape(leading, KV_HEADS * group_size * 2 * HD)


def local(
    passage_states,
    question_states,
    norm_gain,
    query_weight,
    kv_weight,
    out_weight,
    passage_ids,
    slot_offsets,
):
    n = lax.axis_size("head")
    pas_rows = passage_states.shape[0]
    question_rows = question_states.shape[0]
    features = norm_gain.shape[0]
    group_size = n // KV_HEADS
    block_cols = kv_weight.shape[1] // n
    query_cols = query_weight.shape[1]

    def normed(states):
        rows = states.astype(jnp.float32)
        return (rows * norm_gain[None, :]).astype(jnp.bfloat16), jnp.sum(rows * rows, axis=1)

    gained_q, squares_q = normed(question_states)
    spread = spread_heads(kv_weight, group_size)
    positions = jnp.arange(passage_ids.shape[1] * PLEN + QLEN, dtype=jnp.int32)
    tables = rope_tables(positions)
    query_sums, passage_sums, request_sums, squares, tables = project(
        gained_q, squares_q, normed, passage_states, tables, query_weight, spread, n
    )
    row_scale = lax.rsqrt(squares / D + 1e-05)[:, None]
    passage_kv = (row_scale[:pas_rows] * passage_sums).astype(jnp.bfloat16)
    request_kv = (row_scale[pas_rows:] * request_sums).astype(jnp.bfloat16)
    own_start = lax.axis_index("head") % group_size * block_cols
    passage_out = lax.dynamic_slice_in_dim(passage_kv, own_start, block_cols, 1)
    items = lax.axis_size("item")
    stored = [passage_kv]
    for _ in range(items - 1):
        ring = [(i, (i - 1) % items) for i in range(items)]
        stored.append(lax.ppermute(stored[-1], "item", ring))
    stored = jnp.concatenate(stored, axis=0)
    held = stored.shape[0] // PLEN
    place = (passage_ids - lax.axis_index("item") * (pas_rows // PLEN)) % held
    def out_block(rows, device):
        columns = lax.dynamic_slice_in_dim(out_weight, device * features, features, 1)
        product = jnp.dot(rows, columns, preferred_element_type=jnp.float32)
        return product.astype(jnp.bfloat16)

    requests = passage_ids.shape[0] // 2

    def attention_of(half, stored):
        rows = slice(half * requests, (half + 1) * requests)
        return attend(
            place[rows],
            slot_offsets[rows],
            query_sums,
            row_scale,
            request_kv,
            stored,
            tables,
            half * requests,
        )

    first = scatter_sum(out_block, attention_of(0, stored), n, stored)
    attention = attention_of(1, next(first))
    second = scatter_sum(out_block, attention, n, None, first.send(attention))
    summed = jnp.concatenate(interleave([second, first])[::-1], axis=0)
    question_out = (question_states.astype(jnp.float32) + summed).astype(jnp.bfloat16)
    return (passage_out, question_out)


def solution(mesh):
    return jax.shard_map(
        local,
        mesh=mesh,
        in_specs=(
            P(("grp", "item"), "head"),
            P(("grp", "item"), "head"),
            P("head"),
            P(None, "head"),
            P("head", None),
            P("head", None),
            P(("grp", "item"), None),
            P(("grp", "item"), None),
        ),
        out_specs=(P(("grp", "item"), "head"), P(("grp", "item"), "head")),
        check_vma=False,
    )
```

```python
import math

import jax
import jax.numpy as jnp
from jax import lax
from jax.experimental import pallas as pl
from jax.experimental.pallas import tpu as pltpu
from jax.sharding import PartitionSpec as P

D = 8192
KV_HEADS = 8
HD = 128
PLEN = 256
QLEN = 128
SIDE = 2


def rope_tables(positions):
    lanes = jnp.arange(HD, dtype=jnp.int32)
    inverse = jnp.exp(
        (lanes % (HD // 2)).astype(jnp.float32) * (-2.0 * math.log(500000.0) / HD)
    )
    angles = positions.astype(jnp.float32)[:, None] * inverse[None, :]
    return jnp.cos(angles), jnp.where(lanes[None, :] < HD // 2, -jnp.sin(angles), jnp.sin(angles))


def attention_kernel(
    ids, offsets, sums, scale, request_kv, stored, cosines, sines, out, turned, keys, values
):
    request = pl.program_id(0)
    slots = ids.shape[1]
    cached = slots * PLEN
    total_keys = cached + QLEN
    heads = sums.shape[1] // HD

    def rot(vectors, cosine, sine):
        return vectors * cosine + pltpu.roll(vectors, HD // 2, 1) * sine

    q_cos = cosines[pl.ds(cached, QLEN), :]
    q_sin = sines[pl.ds(cached, QLEN), :]
    for slot in range(slots):
        start = pl.multiple_of(ids[request, slot] * PLEN, PLEN)
        offset = offsets[request, slot]
        rows = slice(slot * PLEN, (slot + 1) * PLEN)
        key = stored[pl.ds(start, PLEN), :HD].astype(jnp.float32)
        key = rot(key, cosines[pl.ds(offset, PLEN), :], sines[pl.ds(offset, PLEN), :])
        keys[rows, :] = key.astype(jnp.bfloat16)
        values[rows, :] = stored[pl.ds(start, PLEN), HD:]
    key = rot(request_kv[:, :HD].astype(jnp.float32), q_cos, q_sin)
    keys[cached:, :] = key.astype(jnp.bfloat16)
    values[cached:, :] = request_kv[:, HD:]
    row_scale = scale[...]
    for head in range(heads):
        query = row_scale * sums[:, head * HD : (head + 1) * HD]
        query = rot(query, q_cos, q_sin) * HD ** (-0.5)
        turned[head * QLEN : (head + 1) * QLEN, :] = query.astype(jnp.bfloat16)
    together = 2 if heads % 2 == 0 else 1
    height = together * QLEN
    row = lax.broadcasted_iota(jnp.int32, (height, QLEN), 0) % QLEN
    allowed = lax.broadcasted_iota(jnp.int32, (height, QLEN), 1) <= row
    for block in range(heads // together):
        scores = lax.dot_general(
            turned[block * height : (block + 1) * height, :],
            keys[...],
            (((1,), (1,)), ((), ())),
            preferred_element_type=jnp.float32,
        )
        own = jnp.where(allowed, scores[:, cached:], -1e30)
        scores = scores[:, :cached]
        row_max = jnp.maximum(
            jnp.max(scores, axis=1, keepdims=True), jnp.max(own, axis=1, keepdims=True)
        )
        weights = jnp.exp(scores - row_max)
        own = jnp.where(allowed, jnp.exp(own - row_max), 0.0)
        total = jnp.sum(weights, axis=1, keepdims=True) + jnp.sum(own, axis=1, keepdims=True)
        blended = jnp.dot(
            weights.astype(jnp.bfloat16), values[:cached, :], preferred_element_type=jnp.float32
        ) + jnp.dot(own.astype(jnp.bfloat16), values[cached:, :], preferred_element_type=jnp.float32)
        blended = (blended / total).astype(jnp.bfloat16)
        for i in range(together):
            head = block * together + i
            out[:, head * HD : (head + 1) * HD] = blended[i * QLEN : (i + 1) * QLEN, :]


def attend(ids, offsets, sums, scale, request_kv, stored, tables, first):
    requests, slots = ids.shape
    rows, cols = requests * QLEN, sums.shape[1]
    total_keys = slots * PLEN + QLEN
    heads = cols // HD

    def per_request(width, skipped=0):
        return pl.BlockSpec((QLEN, width), lambda r, *_: (skipped + first + r, 0))

    def whole(array):
        return pl.BlockSpec(array.shape, lambda r, *_: (0, 0))

    return pl.pallas_call(
        attention_kernel,
        grid_spec=pltpu.PrefetchScalarGridSpec(
            num_scalar_prefetch=2,
            grid=(requests,),
            in_specs=[
                per_request(cols),
                per_request(1, (scale.shape[0] - sums.shape[0]) // QLEN),
                per_request(2 * HD),
                whole(stored),
                whole(tables[0]),
                whole(tables[1]),
            ],
            out_specs=pl.BlockSpec((QLEN, cols), lambda r, *_: (r, 0)),
            scratch_shapes=[
                pltpu.VMEM((heads * QLEN, HD), jnp.bfloat16),
                pltpu.VMEM((total_keys, HD), jnp.bfloat16),
                pltpu.VMEM((total_keys, HD), jnp.bfloat16),
            ],
        ),
        out_shape=jax.ShapeDtypeStruct((rows, cols), jnp.bfloat16),
        compiler_params=pltpu.CompilerParams(vmem_limit_bytes=32 * 1024 * 1024),
        cost_estimate=pl.CostEstimate(flops=1, bytes_accessed=1, transcendentals=0),
        name="attention",
    )(ids, offsets, sums, scale, request_kv, stored, *tables)


def swap(value, n, link, distance=None):
    depth = n // SIDE
    perm = []
    for z in range(depth):
        way = 1 if z % 2 == link else -1
        if 0 <= z + way < depth and (distance is None or 0 <= z + way * distance < depth):
            perm += [(z * SIDE + y, (z + way) * SIDE + y) for y in range(SIDE)]
    return lax.ppermute(value, "head", perm)


def cross(value, n):
    return lax.ppermute(value, "head", [(h, h ^ 1) for h in range(n)])


def pick(index, choices):
    arrays = []
    for choice in choices:
        if choice is not None and not any(choice is a for a in arrays):
            arrays.append(choice)
    result = arrays[0]
    for array in arrays[1:]:
        mask = False
        for i, choice in enumerate(choices):
            if choice is array:
                mask = mask | (index == i)
        result = jnp.where(mask, array, result)
    return result


def table_at(index, values):
    result = jnp.int32(values[-1])
    for i in range(len(values) - 1):
        result = jnp.where(index == i, jnp.int32(values[i]), result)
    return result


def orders(depth):
    def key(z, d):
        return -abs(d - z), (d > z) == (z % 2 == 0)

    return [sorted(range(depth), key=lambda d, z=z: key(z, d)) for z in range(depth)]


def arrivals(depth):
    result = []
    for z in range(depth):
        near = []
        for s in range(1, depth):
            for link in range(2):
                way = 1 if z % 2 == link else -1
                if 0 <= z + way * s < depth:
                    near.append((s, link))
        result.append(near)
    return result


def tie(*trees):
    return lax.optimization_barrier(trees)


def fold(rows, height):
    if rows.shape[0] == height:
        return rows
    return jnp.concatenate(jnp.split(rows, rows.shape[0] // height, axis=0), axis=1)


def unfold(block, cols):
    if block.shape[1] == cols:
        return block
    return jnp.concatenate(jnp.split(block, block.shape[1] // cols, axis=1), axis=0)


def widen(array, cols):
    if array.shape[1] == cols:
        return array
    return jnp.pad(array, ((0, 0), (0, cols - array.shape[1])))


def join(arrays):
    return arrays[0] if len(arrays) == 1 else jnp.concatenate(arrays, axis=1)


def line_values(z, depth, slots, k, came):
    order = orders(depth)
    values = []
    for link in range(2):
        chosen = []
        for zz in range(depth):
            d = zz + k if zz % 2 == link else zz - k
            chosen.append(slots[order[zz].index(d)] if 0 <= d < depth else None)
        if all(c is None for c in chosen):
            continue
        value = pick(z, chosen)
        if len(came) > 1 - link:
            value = value + came[1 - link].astype(jnp.float32)
        values.append(value.astype(jnp.bfloat16))
    return values


def project(part, squares_q, normed, passages, tables, query_weight, kv_weight, n):
    depth = n // SIDE
    height, features = part.shape
    cols = 2 * HD
    me = lax.axis_index("head")
    z, y = me // SIDE, me % SIDE
    other = 1 - y
    order = orders(depth)
    near = arrivals(depth)
    dest = [table_at(z, [order[zz][slot] for zz in range(depth)]) for slot in range(depth)]
    blocks = passages.shape[0] // height
    width = max(features, blocks * SIDE * cols)
    behind = [jnp.where(z % 2 == link, z, depth - 1 - z) for link in range(2)]

    def product(total, news):
        for came, owner in news:
            rows = lax.dynamic_slice_in_dim(query_weight, owner * features, features, 0)
            term = jnp.dot(came, rows, preferred_element_type=jnp.float32)
            total = term if total is None else total + term
        return total

    def kv_product(rows, start, count):
        weight = lax.dynamic_slice_in_dim(kv_weight, start, count, 1)
        return jnp.dot(rows, weight, preferred_element_type=jnp.float32)

    went = [[part, part]]
    crossing = (part, z)
    total, news = None, [(part, me)]
    squares, partner = squares_q, 1
    p_slots, p_came = [], ()
    q_slots, q_came, q_give = [], (), None
    questions = part
    for t in range(1, depth + 2):
        to_y, to_z = [], [[], []]
        if t <= depth:
            to_y.append(crossing[0])
        if t == 1:
            to_z = [[widen(part, width)], [widen(part, width)]]
        elif t <= depth:
            values = line_values(z, depth, p_slots, depth - t + 1, p_came)
            for link in range(2):
                payload = widen(went[-1][1 - link], width)
                if link < len(values):
                    mine = widen(fold(values[link], height), width)
                    payload = jnp.where(behind[link] < t - 1, mine, payload)
                to_z[link].append(payload)
        else:
            p_total = p_slots[depth - 1]
            for array in p_came:
                p_total = p_total + array.astype(jnp.float32)
            left, right = jnp.split(p_total, 2, axis=1)
            p_keep = jnp.where(y == 0, left, right)
            to_y.append(fold(jnp.where(y == 0, right, left).astype(jnp.bfloat16), height))
        alone = [q_give] if t >= 2 else []
        if t >= 3:
            values = line_values(z, depth, q_slots, depth - t + 2, q_came)
            for link, value in enumerate(values):
                to_z[link].append(value)
        sends, late, news_arrays, total, passages, questions, p_slots, q_slots = tie(
            [join(to_y), join(to_z[0]), join(to_z[1])] + alone,
            [squares] if t >= 2 else [],
            [came for came, _ in news],
            [] if total is None else [total],
            passages,
            questions,
            p_slots,
            q_slots,
        )
        received = [cross(sends[0], n), swap(sends[1], n, 0), swap(sends[2], n, 1)]
        if late:
            squares = late[0]
        summing = t >= 2 and partner < n
        q_came_y = [cross(array, n) for array in sends[3:]]
        if t == 1:
            passages, squares_p = normed(passages)
            squares = jnp.concatenate([squares_p, squares])
        total = product(total[0] if total else None, [(c, o) for c, (_, o) in zip(news_arrays, news)])
        new_p = [kv_product(passages, dest[t - 1] * SIDE * cols, SIDE * cols)] if t <= depth else []
        if summing and new_p:
            squares, total = tie(squares, total)
        if summing:
            received.append(lax.ppermute(squares, "head", [(h, h ^ partner) for h in range(n)]))
        q_mine = []
        if t >= 2:
            q_mine = [kv_product(questions, (dest[t - 2] * SIDE + y) * cols, cols)]
        new_give = []
        if t <= depth:
            new_give = [
                kv_product(questions, (dest[t - 1] * SIDE + other) * cols, cols).astype(jnp.bfloat16)
            ]
        received, q_came_y, squares, total, new_p, q_mine, new_give = tie(
            received, q_came_y, squares, total, new_p, q_mine, new_give
        )
        if t == 2:
            received, tables = tie(received, tables)
        if summing:
            squares = squares + received.pop()
            partner *= 2
        p_slots = p_slots + new_p
        q_give = new_give[0] if new_give else None
        news = []
        if t <= depth:
            news.append((received[0][:, :features], crossing[1] * SIDE + other))
        else:
            p_came_y = unfold(received[0], cols)
        if t >= 2:
            q_slots = q_slots + [q_mine[0] + q_came_y[0].astype(jnp.float32)]
        if t < depth:
            went.append([array[:, :features] for array in received[1:]])
            slot = [near[zz][t - 1] for zz in range(depth)]
            came = pick(z, [went[s][link] for s, link in slot])
            source = table_at(
                z, [zz + s if zz % 2 == link else zz - s for zz, (s, link) in enumerate(slot)]
            )
            crossing = (came, source)
            news.append((came, source * SIDE + y))
        if 2 <= t <= depth:
            used = blocks * SIDE * cols
            p_came = [unfold(array[:, :used], SIDE * cols) for array in received[1:]]
        if t >= 3:
            q_came = [array[:, (width if t <= depth else 0) :] for array in received[1:]]
            q_came = [array for array in q_came if array.shape[1]]
    q_total = q_slots[depth - 1]
    for array in q_came:
        q_total = q_total + array.astype(jnp.float32)
    passage_sums = p_keep + p_came_y.astype(jnp.float32)
    return product(total, news), passage_sums, q_total, squares, tables


def scatter_sum(block_of, source, n, held=None, later=None):
    depth = n // SIDE
    me = lax.axis_index("head")
    z, y = me // SIDE, me % SIDE
    order = orders(depth)
    dest = [
        table_at(z, [order[zz][slot] for zz in range(depth)]) * SIDE for slot in range(depth)
    ]
    slots, came = [], []
    give = block_of(source, dest[0] + 1 - y)
    source = source if later is None else later
    for turn in range(depth):
        sends = [give]
        if turn:
            sends += line_values(z, depth, slots, depth - turn, came)
        sends, source, slots, held = tie(sends, source, slots, held)
        received = [cross(sends[0], n)]
        for link, value in enumerate(sends[1:]):
            received.append(swap(value, n, link, depth - turn))
        mine = block_of(source, dest[turn] + y)
        gives = []
        if turn + 1 < depth:
            gives = [block_of(source, dest[turn + 1] + 1 - y)]
        held = yield held
        received, mine, gives, held = tie(received, mine, gives, held)
        give = gives[0] if gives else None
        came = received[1:]
        slots = slots + [mine.astype(jnp.float32) + received[0].astype(jnp.float32)]
    total = slots[depth - 1]
    for array in came:
        total = total + array.astype(jnp.float32)
    return total


def interleave(generators):
    results = [None] * len(generators)
    live = list(range(len(generators)))
    while live:
        for i in list(live):
            try:
                next(generators[i])
            except StopIteration as stop:
                results[i] = stop.value
                live.remove(i)
    return results


def spread_heads(matrix, group_size):
    if group_size == 1:
        return matrix
    leading = matrix.shape[0]
    per_head = matrix.reshape(leading, KV_HEADS, 2 * HD)
    return jnp.repeat(per_head, group_size, axis=1).reshape(leading, KV_HEADS * group_size * 2 * HD)


def local(
    passage_states,
    question_states,
    norm_gain,
    query_weight,
    kv_weight,
    out_weight,
    passage_ids,
    slot_offsets,
):
    n = lax.axis_size("head")
    pas_rows = passage_states.shape[0]
    question_rows = question_states.shape[0]
    features = norm_gain.shape[0]
    group_size = n // KV_HEADS
    block_cols = kv_weight.shape[1] // n
    query_cols = query_weight.shape[1]

    def normed(states):
        rows = states.astype(jnp.float32)
        return (rows * norm_gain[None, :]).astype(jnp.bfloat16), jnp.sum(rows * rows, axis=1)

    gained_q, squares_q = normed(question_states)
    spread = spread_heads(kv_weight, group_size)
    positions = jnp.arange(passage_ids.shape[1] * PLEN + QLEN, dtype=jnp.int32)
    tables = rope_tables(positions)
    query_sums, passage_sums, request_sums, squares, tables = project(
        gained_q, squares_q, normed, passage_states, tables, query_weight, spread, n
    )
    row_scale = lax.rsqrt(squares / D + 1e-05)[:, None]
    passage_kv = (row_scale[:pas_rows] * passage_sums).astype(jnp.bfloat16)
    request_kv = (row_scale[pas_rows:] * request_sums).astype(jnp.bfloat16)
    own_start = lax.axis_index("head") % group_size * block_cols
    passage_out = lax.dynamic_slice_in_dim(passage_kv, own_start, block_cols, 1)
    items = lax.axis_size("item")
    stored = [passage_kv]
    for _ in range(items - 1):
        ring = [(i, (i - 1) % items) for i in range(items)]
        stored.append(lax.ppermute(stored[-1], "item", ring))
    stored = jnp.concatenate(stored, axis=0)
    held = stored.shape[0] // PLEN
    place = (passage_ids - lax.axis_index("item") * (pas_rows // PLEN)) % held
    def out_block(rows, device):
        columns = lax.dynamic_slice_in_dim(out_weight, device * features, features, 1)
        product = jnp.dot(rows, columns, preferred_element_type=jnp.float32)
        return product.astype(jnp.bfloat16)

    requests = passage_ids.shape[0] // 2

    def attention_of(half, stored):
        rows = slice(half * requests, (half + 1) * requests)
        return attend(
            place[rows],
            slot_offsets[rows],
            query_sums,
            row_scale,
            request_kv,
            stored,
            tables,
            half * requests,
        )

    first = scatter_sum(out_block, attention_of(0, stored), n, stored)
    attention = attention_of(1, next(first))
    second = scatter_sum(out_block, attention, n, None, first.send(attention))
    summed = jnp.concatenate(interleave([second, first])[::-1], axis=0)
    question_out = (question_states.astype(jnp.float32) + summed).astype(jnp.bfloat16)
    return (passage_out, question_out)


def solution(mesh):
    return jax.shard_map(
        local,
        mesh=mesh,
        in_specs=(
            P(("grp", "item"), "head"),
            P(("grp", "item"), "head"),
            P("head"),
            P(None, "head"),
            P("head", None),
            P("head", None),
            P(("grp", "item"), None),
            P(("grp", "item"), None),
        ),
        out_specs=(P(("grp", "item"), "head"), P(("grp", "item"), "head")),
        check_vma=False,
    )
```

```python
import math

import jax
import jax.numpy as jnp
from jax import lax
from jax.experimental import pallas as pl
from jax.experimental.pallas import tpu as pltpu
from jax.sharding import PartitionSpec as P

D = 8192
KV_HEADS = 8
HD = 128
PLEN = 256
QLEN = 128
SIDE = 2


def rope_tables(positions):
    lanes = jnp.arange(HD, dtype=jnp.int32)
    inverse = jnp.exp(
        (lanes % (HD // 2)).astype(jnp.float32) * (-2.0 * math.log(500000.0) / HD)
    )
    angles = positions.astype(jnp.float32)[:, None] * inverse[None, :]
    return jnp.cos(angles), jnp.where(lanes[None, :] < HD // 2, -jnp.sin(angles), jnp.sin(angles))


def attention_kernel(
    ids, offsets, sums, scale, request_kv, stored, cosines, sines, out, turned, keys, values
):
    request = pl.program_id(0)
    slots = ids.shape[1]
    cached = slots * PLEN
    total_keys = cached + QLEN
    heads = sums.shape[1] // HD

    def rot(vectors, cosine, sine):
        return vectors * cosine + pltpu.roll(vectors, HD // 2, 1) * sine

    q_cos = cosines[pl.ds(cached, QLEN), :]
    q_sin = sines[pl.ds(cached, QLEN), :]
    for slot in range(slots):
        start = pl.multiple_of(ids[request, slot] * PLEN, PLEN)
        offset = offsets[request, slot]
        rows = slice(slot * PLEN, (slot + 1) * PLEN)
        key = stored[pl.ds(start, PLEN), :HD].astype(jnp.float32)
        key = rot(key, cosines[pl.ds(offset, PLEN), :], sines[pl.ds(offset, PLEN), :])
        keys[rows, :] = key.astype(jnp.bfloat16)
        values[rows, :] = stored[pl.ds(start, PLEN), HD:]
    key = rot(request_kv[:, :HD].astype(jnp.float32), q_cos, q_sin)
    keys[cached:, :] = key.astype(jnp.bfloat16)
    values[cached:, :] = request_kv[:, HD:]
    row_scale = scale[...]
    for head in range(heads):
        query = row_scale * sums[:, head * HD : (head + 1) * HD]
        query = rot(query, q_cos, q_sin) * HD ** (-0.5)
        turned[head * QLEN : (head + 1) * QLEN, :] = query.astype(jnp.bfloat16)
    together = 2 if heads % 2 == 0 else 1
    height = together * QLEN
    row = lax.broadcasted_iota(jnp.int32, (height, QLEN), 0) % QLEN
    allowed = lax.broadcasted_iota(jnp.int32, (height, QLEN), 1) <= row
    for block in range(heads // together):
        scores = lax.dot_general(
            turned[block * height : (block + 1) * height, :],
            keys[...],
            (((1,), (1,)), ((), ())),
            preferred_element_type=jnp.float32,
        )
        own = jnp.where(allowed, scores[:, cached:], -1e30)
        scores = scores[:, :cached]
        row_max = jnp.maximum(
            jnp.max(scores, axis=1, keepdims=True), jnp.max(own, axis=1, keepdims=True)
        )
        weights = jnp.exp(scores - row_max)
        own = jnp.where(allowed, jnp.exp(own - row_max), 0.0)
        total = jnp.sum(weights, axis=1, keepdims=True) + jnp.sum(own, axis=1, keepdims=True)
        blended = jnp.dot(
            weights.astype(jnp.bfloat16), values[:cached, :], preferred_element_type=jnp.float32
        ) + jnp.dot(own.astype(jnp.bfloat16), values[cached:, :], preferred_element_type=jnp.float32)
        blended = (blended / total).astype(jnp.bfloat16)
        for i in range(together):
            head = block * together + i
            out[:, head * HD : (head + 1) * HD] = blended[i * QLEN : (i + 1) * QLEN, :]


def attend(ids, offsets, sums, scale, request_kv, stored, tables, first):
    requests, slots = ids.shape
    rows, cols = requests * QLEN, sums.shape[1]
    total_keys = slots * PLEN + QLEN
    heads = cols // HD

    def per_request(width, skipped=0):
        return pl.BlockSpec((QLEN, width), lambda r, *_: (skipped + first + r, 0))

    def whole(array):
        return pl.BlockSpec(array.shape, lambda r, *_: (0, 0))

    return pl.pallas_call(
        attention_kernel,
        grid_spec=pltpu.PrefetchScalarGridSpec(
            num_scalar_prefetch=2,
            grid=(requests,),
            in_specs=[
                per_request(cols),
                per_request(1, (scale.shape[0] - sums.shape[0]) // QLEN),
                per_request(2 * HD),
                whole(stored),
                whole(tables[0]),
                whole(tables[1]),
            ],
            out_specs=pl.BlockSpec((QLEN, cols), lambda r, *_: (r, 0)),
            scratch_shapes=[
                pltpu.VMEM((heads * QLEN, HD), jnp.bfloat16),
                pltpu.VMEM((total_keys, HD), jnp.bfloat16),
                pltpu.VMEM((total_keys, HD), jnp.bfloat16),
            ],
        ),
        out_shape=jax.ShapeDtypeStruct((rows, cols), jnp.bfloat16),
        compiler_params=pltpu.CompilerParams(vmem_limit_bytes=32 * 1024 * 1024),
        cost_estimate=pl.CostEstimate(flops=1, bytes_accessed=1, transcendentals=0),
        name="attention",
    )(ids, offsets, sums, scale, request_kv, stored, *tables)


def swap(value, n, link, distance=None):
    depth = n // SIDE
    perm = []
    for z in range(depth):
        way = 1 if z % 2 == link else -1
        if 0 <= z + way < depth and (distance is None or 0 <= z + way * distance < depth):
            perm += [(z * SIDE + y, (z + way) * SIDE + y) for y in range(SIDE)]
    return lax.ppermute(value, "head", perm)


def cross(value, n):
    return lax.ppermute(value, "head", [(h, h ^ 1) for h in range(n)])


def pick(index, choices):
    arrays = []
    for choice in choices:
        if choice is not None and not any(choice is a for a in arrays):
            arrays.append(choice)
    result = arrays[0]
    for array in arrays[1:]:
        mask = False
        for i, choice in enumerate(choices):
            if choice is array:
                mask = mask | (index == i)
        result = jnp.where(mask, array, result)
    return result


def table_at(index, values):
    result = jnp.int32(values[-1])
    for i in range(len(values) - 1):
        result = jnp.where(index == i, jnp.int32(values[i]), result)
    return result


def orders(depth):
    def key(z, d):
        return -abs(d - z), (d > z) == (z % 2 == 0)

    return [sorted(range(depth), key=lambda d, z=z: key(z, d)) for z in range(depth)]


def arrivals(depth):
    result = []
    for z in range(depth):
        near = []
        for s in range(1, depth):
            for link in range(2):
                way = 1 if z % 2 == link else -1
                if 0 <= z + way * s < depth:
                    near.append((s, link))
        result.append(near)
    return result


def tie(*trees):
    return lax.optimization_barrier(trees)


def fold(rows, height):
    if rows.shape[0] == height:
        return rows
    return jnp.concatenate(jnp.split(rows, rows.shape[0] // height, axis=0), axis=1)


def unfold(block, cols):
    if block.shape[1] == cols:
        return block
    return jnp.concatenate(jnp.split(block, block.shape[1] // cols, axis=1), axis=0)


def widen(array, cols):
    if array.shape[1] == cols:
        return array
    return jnp.pad(array, ((0, 0), (0, cols - array.shape[1])))


def join(arrays):
    return arrays[0] if len(arrays) == 1 else jnp.concatenate(arrays, axis=1)


def line_values(z, depth, slots, k, came):
    order = orders(depth)
    values = []
    for link in range(2):
        chosen = []
        for zz in range(depth):
            d = zz + k if zz % 2 == link else zz - k
            chosen.append(slots[order[zz].index(d)] if 0 <= d < depth else None)
        if all(c is None for c in chosen):
            continue
        value = pick(z, chosen)
        if len(came) > 1 - link:
            value = value + came[1 - link].astype(jnp.float32)
        values.append(value.astype(jnp.bfloat16))
    return values


def project(part, squares_q, normed, passages, tables, query_weight, kv_weight, n):
    depth = n // SIDE
    height, features = part.shape
    cols = 2 * HD
    me = lax.axis_index("head")
    z, y = me // SIDE, me % SIDE
    other = 1 - y
    order = orders(depth)
    near = arrivals(depth)
    dest = [table_at(z, [order[zz][slot] for zz in range(depth)]) for slot in range(depth)]
    blocks = passages.shape[0] // height
    width = max(features, blocks * SIDE * cols)
    behind = [jnp.where(z % 2 == link, z, depth - 1 - z) for link in range(2)]

    def product(total, news):
        for came, owner in news:
            rows = lax.dynamic_slice_in_dim(query_weight, owner * features, features, 0)
            term = jnp.dot(came, rows, preferred_element_type=jnp.float32)
            total = term if total is None else total + term
        return total

    def kv_product(rows, start, count):
        weight = lax.dynamic_slice_in_dim(kv_weight, start, count, 1)
        return jnp.dot(rows, weight, preferred_element_type=jnp.float32)

    went = [[part, part]]
    crossing = (part, z)
    total, news = None, [(part, me)]
    squares, partner = squares_q, 1
    p_slots, p_came = [], ()
    q_slots, q_came, q_give = [], (), None
    questions = part
    for t in range(1, depth + 2):
        to_y, to_z = [], [[], []]
        if t <= depth:
            to_y.append(crossing[0])
        if t == 1:
            to_z = [[widen(part, width)], [widen(part, width)]]
        elif t <= depth:
            values = line_values(z, depth, p_slots, depth - t + 1, p_came)
            for link in range(2):
                payload = widen(went[-1][1 - link], width)
                if link < len(values):
                    mine = widen(fold(values[link], height), width)
                    payload = jnp.where(behind[link] < t - 1, mine, payload)
                to_z[link].append(payload)
        else:
            p_total = p_slots[depth - 1]
            for array in p_came:
                p_total = p_total + array.astype(jnp.float32)
            left, right = jnp.split(p_total, 2, axis=1)
            p_keep = jnp.where(y == 0, left, right)
            to_y.append(fold(jnp.where(y == 0, right, left).astype(jnp.bfloat16), height))
        alone = [q_give] if t >= 2 else []
        if t >= 3:
            values = line_values(z, depth, q_slots, depth - t + 2, q_came)
            for link, value in enumerate(values):
                to_z[link].append(value)
        sends, late, news_arrays, total, passages, questions, p_slots, q_slots = tie(
            [join(to_y), join(to_z[0]), join(to_z[1])] + alone,
            [squares] if t >= 2 else [],
            [came for came, _ in news],
            [] if total is None else [total],
            passages,
            questions,
            p_slots,
            q_slots,
        )
        by_line = [swap(sends[1 + link], n, link) for link in range(2)]
        received = [cross(sends[0], n)] + by_line
        if late:
            squares = late[0]
        summing = t >= 2 and partner < n
        q_came_y = [cross(array, n) for array in sends[3:]]
        if t == 1:
            passages, squares_p = normed(passages)
            squares = jnp.concatenate([squares_p, squares])
        total = product(total[0] if total else None, [(c, o) for c, (_, o) in zip(news_arrays, news)])
        new_p = [kv_product(passages, dest[t - 1] * SIDE * cols, SIDE * cols)] if t <= depth else []
        if summing and new_p:
            squares, total = tie(squares, total)
        if summing:
            received.append(lax.ppermute(squares, "head", [(h, h ^ partner) for h in range(n)]))
        q_mine = []
        if t >= 2:
            q_mine = [kv_product(questions, (dest[t - 2] * SIDE + y) * cols, cols)]
        new_give = []
        if t <= depth:
            new_give = [
                kv_product(questions, (dest[t - 1] * SIDE + other) * cols, cols).astype(jnp.bfloat16)
            ]
        received, q_came_y, squares, total, new_p, q_mine, new_give = tie(
            received, q_came_y, squares, total, new_p, q_mine, new_give
        )
        if t == 2:
            received, tables = tie(received, tables)
        if summing:
            squares = squares + received.pop()
            partner *= 2
        p_slots = p_slots + new_p
        q_give = new_give[0] if new_give else None
        news = []
        if t <= depth:
            news.append((received[0][:, :features], crossing[1] * SIDE + other))
        else:
            p_came_y = unfold(received[0], cols)
        if t >= 2:
            q_slots = q_slots + [q_mine[0] + q_came_y[0].astype(jnp.float32)]
        if t < depth:
            went.append([array[:, :features] for array in received[1:]])
            slot = [near[zz][t - 1] for zz in range(depth)]
            came = pick(z, [went[s][link] for s, link in slot])
            source = table_at(
                z, [zz + s if zz % 2 == link else zz - s for zz, (s, link) in enumerate(slot)]
            )
            crossing = (came, source)
            news.append((came, source * SIDE + y))
        if 2 <= t <= depth:
            used = blocks * SIDE * cols
            p_came = [unfold(array[:, :used], SIDE * cols) for array in received[1:]]
        if t >= 3:
            q_came = [array[:, (width if t <= depth else 0) :] for array in received[1:]]
            q_came = [array for array in q_came if array.shape[1]]
    q_total = q_slots[depth - 1]
    for array in q_came:
        q_total = q_total + array.astype(jnp.float32)
    passage_sums = p_keep + p_came_y.astype(jnp.float32)
    return product(total, news), passage_sums, q_total, squares, tables


def scatter_sum(block_of, source, n, held=None, later=None):
    depth = n // SIDE
    me = lax.axis_index("head")
    z, y = me // SIDE, me % SIDE
    order = orders(depth)
    dest = [
        table_at(z, [order[zz][slot] for zz in range(depth)]) * SIDE for slot in range(depth)
    ]
    slots, came = [], []
    give = block_of(source, dest[0] + 1 - y)
    source = source if later is None else later
    for turn in range(depth):
        sends = [give]
        if turn:
            sends += line_values(z, depth, slots, depth - turn, came)
        sends, source, slots, held = tie(sends, source, slots, held)
        received = [cross(sends[0], n)]
        for link, value in enumerate(sends[1:]):
            received.append(swap(value, n, link, depth - turn))
        mine = block_of(source, dest[turn] + y)
        gives = []
        if turn + 1 < depth:
            gives = [block_of(source, dest[turn + 1] + 1 - y)]
        held = yield held
        received, mine, gives, held = tie(received, mine, gives, held)
        give = gives[0] if gives else None
        came = received[1:]
        slots = slots + [mine.astype(jnp.float32) + received[0].astype(jnp.float32)]
    total = slots[depth - 1]
    for array in came:
        total = total + array.astype(jnp.float32)
    return total


def interleave(generators):
    results = [None] * len(generators)
    live = list(range(len(generators)))
    while live:
        for i in list(live):
            try:
                next(generators[i])
            except StopIteration as stop:
                results[i] = stop.value
                live.remove(i)
    return results


def spread_heads(matrix, group_size):
    if group_size == 1:
        return matrix
    leading = matrix.shape[0]
    per_head = matrix.reshape(leading, KV_HEADS, 2 * HD)
    return jnp.repeat(per_head, group_size, axis=1).reshape(leading, KV_HEADS * group_size * 2 * HD)


def local(
    passage_states,
    question_states,
    norm_gain,
    query_weight,
    kv_weight,
    out_weight,
    passage_ids,
    slot_offsets,
):
    n = lax.axis_size("head")
    pas_rows = passage_states.shape[0]
    question_rows = question_states.shape[0]
    features = norm_gain.shape[0]
    group_size = n // KV_HEADS
    block_cols = kv_weight.shape[1] // n
    query_cols = query_weight.shape[1]

    def normed(states):
        rows = states.astype(jnp.float32)
        return (rows * norm_gain[None, :]).astype(jnp.bfloat16), jnp.sum(rows * rows, axis=1)

    gained_q, squares_q = normed(question_states)
    spread = spread_heads(kv_weight, group_size)
    positions = jnp.arange(passage_ids.shape[1] * PLEN + QLEN, dtype=jnp.int32)
    tables = rope_tables(positions)
    query_sums, passage_sums, request_sums, squares, tables = project(
        gained_q, squares_q, normed, passage_states, tables, query_weight, spread, n
    )
    row_scale = lax.rsqrt(squares / D + 1e-05)[:, None]
    passage_kv = (row_scale[:pas_rows] * passage_sums).astype(jnp.bfloat16)
    request_kv = (row_scale[pas_rows:] * request_sums).astype(jnp.bfloat16)
    own_start = lax.axis_index("head") % group_size * block_cols
    passage_out = lax.dynamic_slice_in_dim(passage_kv, own_start, block_cols, 1)
    items = lax.axis_size("item")
    stored = [passage_kv]
    for _ in range(items - 1):
        ring = [(i, (i - 1) % items) for i in range(items)]
        stored.append(lax.ppermute(stored[-1], "item", ring))
    stored = jnp.concatenate(stored, axis=0)
    held = stored.shape[0] // PLEN
    place = (passage_ids - lax.axis_index("item") * (pas_rows // PLEN)) % held
    def out_block(rows, device):
        columns = lax.dynamic_slice_in_dim(out_weight, device * features, features, 1)
        product = jnp.dot(rows, columns, preferred_element_type=jnp.float32)
        return product.astype(jnp.bfloat16)

    requests = passage_ids.shape[0] // 2

    def attention_of(half, stored):
        rows = slice(half * requests, (half + 1) * requests)
        return attend(
            place[rows],
            slot_offsets[rows],
            query_sums,
            row_scale,
            request_kv,
            stored,
            tables,
            half * requests,
        )

    first = scatter_sum(out_block, attention_of(0, stored), n, stored)
    attention = attention_of(1, next(first))
    second = scatter_sum(out_block, attention, n, None, first.send(attention))
    summed = jnp.concatenate(interleave([second, first])[::-1], axis=0)
    question_out = (question_states.astype(jnp.float32) + summed).astype(jnp.bfloat16)
    return (passage_out, question_out)


def solution(mesh):
    return jax.shard_map(
        local,
        mesh=mesh,
        in_specs=(
            P(("grp", "item"), "head"),
            P(("grp", "item"), "head"),
            P("head"),
            P(None, "head"),
            P("head", None),
            P("head", None),
            P(("grp", "item"), None),
            P(("grp", "item"), None),
        ),
        out_specs=(P(("grp", "item"), "head"), P(("grp", "item"), "head")),
        check_vma=False,
    )
```
